32 devices in a mesh: tile: 8 (over z, x), tm: 4 (over y, core).
Axes of the slice: x: 2, y: 2, z: 4, core: 2. Of those that a mesh axis runs over, the one named last changes fastest.
Arguments:
- volume: bfloat16 [16, 64, 16, 128], P('tm', 'tile'), may hold values from -6 to 6
- frame_index: int32 [16], P('tm'), may hold values from 0 to 31, as said below
- tile_offset: int32 [3], replicated, may hold values from 0 to 255
- conv_first: bfloat16 [16, 1, 3, 3, 3], replicated, may hold values from -1.25 to 1.25
- conv_second: bfloat16 [16, 16, 3, 3, 3], replicated, may hold values from -0.3125 to 0.3125
- patch_weight: bfloat16 [8192, 1024], replicated, may hold values from -0.5 to 0.5
- attend_weight: bfloat16 [1024, 3072], P(None, 'tile')
- mixing_weight: bfloat16 [1024, 1024], P(None, 'tile'), may hold values from -0.1875 to 0.1875
- cube_output_projector: bfloat16 [1024, 512], replicated, may hold values from -0.1875 to 0.1875
Outputs:
- prediction_tensor: bfloat16 [16, 8, 2, 16, 512], P('tm', 'tile')
The draws below stay inside these ranges and needn't reach their ends.
Inputs may be any that keep to these rules, and one draw needn't show every extreme that they name: `frame_index`: strictly increasing; the first frame is 0 and the last is 31.
All inputs are finite; a program needn't handle non-finite values.
Results may differ from the reference program's by a relative error of at most 0.015.
Values may be sent and summed in bfloat16 or wider, within the bound.
A program may use at most 256 MiB of HBM per device.

```python
import math
import jax
import jax.numpy as jnp
from jax import lax

CH = 16
D = 1024
HEADS = 8
HD = 128
BLOCK_EDGE_UNITS = 8
PRIOR_SNAPSHOTS = 16
UNITS_DOWNWARD = 16
UNITS_LENGTHWAYS = 128
UNITS_WIDEWAYS = 64
PV = 512
N_TILE = 8


def draw_frame_index(key, part):
    chosen = jax.random.permutation(key, 2 * PRIOR_SNAPSHOTS - 2) + 1
    middle = jnp.sort(chosen[:PRIOR_SNAPSHOTS - 2]).astype(jnp.int32)
    return jnp.concatenate([jnp.zeros((1,), jnp.int32), middle, jnp.full((1,), 2 * PRIOR_SNAPSHOTS - 1, jnp.int32)])


def draw_attend_weight(key, part):
    matrix = jax.random.normal(key, (D, 3 * D), jnp.float32) * D ** (-0.5)
    return matrix.astype(jnp.bfloat16)


def block_scale(rng, dims, pieces, least, high):
    loudness, own = 1.0, jax.random.fold_in(rng, 6)
    for position, shards_of in pieces:
        heights = jnp.exp(jax.random.uniform(jax.random.fold_in(own, position), (shards_of,), jnp.float32, least / len(pieces), high / len(pieces)))
        loudness = loudness * jnp.repeat(heights, dims[position] // shards_of).reshape([-1 if axis == position else 1 for axis in range(len(dims))])
    return loudness


def scatter_about(stream_key, dims, spread, reach, split=(), kind=jnp.bfloat16):
    array = spread * jax.random.normal(stream_key, dims, jnp.float32)
    if split:
        array = array * block_scale(stream_key, dims, split, -0.22, 0.18)
    return jnp.clip(array, -reach, reach).astype(kind)


def setup_inputs(seed: int = 0) -> dict:
    key_of = jax.random.split(jax.random.key(seed), 10)
    return {
        "volume": scatter_about(key_of[0], (PRIOR_SNAPSHOTS, UNITS_WIDEWAYS, UNITS_DOWNWARD, UNITS_LENGTHWAYS), 1.0, 6.0, ((0, 4), (1, 8))),
        "frame_index": draw_frame_index(jax.random.fold_in(key_of[9], 71), 0),
        "tile_offset": jax.random.randint(key_of[2], (3,), 0, 256).astype(jnp.int32),
        "conv_first": scatter_about(key_of[3], (CH, 1, 3, 3, 3), 27 ** -0.5, 1.25),
        "conv_second": scatter_about(key_of[4], (CH, CH, 3, 3, 3), (27 * CH) ** -0.5, 0.3125),
        "patch_weight": scatter_about(key_of[5], (CH * PV, D), (CH * PV // 64) ** -0.5, 0.5),
        "attend_weight": draw_attend_weight(jax.random.fold_in(key_of[9], 71), 0),
        "mixing_weight": scatter_about(key_of[7], (D, D), D ** -0.5, 0.1875, ((1, 8),)),
        "cube_output_projector": scatter_about(key_of[8], (D, PV), D ** -0.5, 0.1875),
    }


def convolve(field_in, kernel):
    return lax.conv_general_dilated(field_in, kernel, (1, 1, 1), ((1, 1), (1, 1), (1, 1)), dimension_numbers=('NCDHW', 'OIDHW', 'NCDHW'), preferred_element_type=jnp.float32)

def settle(values_in):
    return values_in * lax.rsqrt(lax.optimization_barrier(jnp.mean(values_in * values_in, axis=-1, keepdims=True)) + 1e-05)

def embed_time(frame_index):
    frequency = jnp.exp(-math.log(1000.0) * jnp.arange(D, dtype=jnp.float32) / D)
    phase_shift = (jnp.arange(D) % 2).astype(jnp.float32) * (math.pi / 2)
    return (jnp.sin(frame_index.astype(jnp.float32)[:, None] * frequency + phase_shift), frequency)

def embed_space(tile_offset, place_x, place_z, place_y, frequency):
    along_x = (tile_offset[0] + BLOCK_EDGE_UNITS * place_x).astype(jnp.float32)
    along_z = (tile_offset[1] + BLOCK_EDGE_UNITS * place_z).astype(jnp.float32)
    along_y = (tile_offset[2] + BLOCK_EDGE_UNITS * place_y).astype(jnp.float32)
    summed = jnp.sin(along_x[:, None, None, None] * frequency) + jnp.sin(along_z[None, :, None, None] * frequency + 1.0)
    summed = summed + jnp.sin(along_y[None, None, :, None] * frequency + 2.0)
    return summed.reshape(-1, D)

def attend_frames(query, keys_all, values_all, first_frame):
    cube_count = keys_all.shape[1]
    scores = jnp.einsum('tnhd,smhd->htnsm', query.astype(jnp.float32), keys_all.astype(jnp.float32)) / math.sqrt(HD)
    scores = scores.reshape(scores.shape[0], query.shape[0], query.shape[1], -1)
    query_frame = first_frame + jnp.arange(query.shape[0])
    allowed = jnp.arange(keys_all.shape[0])[None, :] <= query_frame[:, None]
    allowed = jnp.repeat(allowed, cube_count, axis=1)
    scores = jnp.where(allowed[None, :, None, :], scores, -1e+30)
    shifted = jnp.exp(scores - lax.optimization_barrier(jnp.max(scores, axis=-1, keepdims=True)))
    weights = (shifted / lax.optimization_barrier(jnp.sum(shifted, axis=-1, keepdims=True))).astype(jnp.bfloat16)
    flat_values = values_all.reshape(-1, values_all.shape[2], values_all.shape[3])
    return jnp.einsum('htnk,khd->tnhd', weights.astype(jnp.float32), flat_values.astype(jnp.float32)).astype(jnp.bfloat16)

def reference(volume, frame_index, tile_offset, conv_first, conv_second, patch_weight, attend_weight, mixing_weight, cube_output_projector):

    def encode(frame_cells):
        first_maps = jax.nn.silu(convolve(frame_cells[None, None], conv_first)).astype(jnp.bfloat16)
        second_maps = jax.nn.silu(convolve(first_maps, conv_second)).astype(jnp.bfloat16)[0]
        patch_cubes = second_maps.reshape(CH, UNITS_WIDEWAYS // BLOCK_EDGE_UNITS, BLOCK_EDGE_UNITS, UNITS_DOWNWARD // BLOCK_EDGE_UNITS, BLOCK_EDGE_UNITS, UNITS_LENGTHWAYS // BLOCK_EDGE_UNITS, BLOCK_EDGE_UNITS)
        patch_cubes = patch_cubes.transpose(1, 3, 5, 0, 2, 4, 6).reshape(-1, CH * BLOCK_EDGE_UNITS ** 3)
        return jnp.dot(patch_cubes, patch_weight, preferred_element_type=jnp.float32)
    encoded = lax.map(encode, volume)
    time_emb, frequency = embed_time(frame_index)
    space_emb = embed_space(tile_offset, jnp.arange(UNITS_WIDEWAYS // BLOCK_EDGE_UNITS), jnp.arange(UNITS_DOWNWARD // BLOCK_EDGE_UNITS), jnp.arange(UNITS_LENGTHWAYS // BLOCK_EDGE_UNITS), frequency)
    tokens = (encoded + time_emb[:, None, :] + space_emb[None]).astype(jnp.bfloat16)
    token_rows = tokens.reshape(-1, D)
    normed = settle(token_rows.astype(jnp.float32)).astype(jnp.bfloat16)
    projected = jnp.dot(normed, attend_weight, preferred_element_type=jnp.float32).astype(jnp.bfloat16)
    projected = projected.reshape(PRIOR_SNAPSHOTS, N_TILE, -1, 3, HEADS, HD).transpose(1, 0, 2, 3, 4, 5)

    def strip_attend(strip_rows):
        return attend_frames(strip_rows[:, :, 0], strip_rows[:, :, 1], strip_rows[:, :, 2], 0)
    attended = lax.map(strip_attend, projected).transpose(1, 0, 2, 3, 4)
    residual = token_rows.astype(jnp.float32) + jnp.dot(attended.reshape(-1, D), mixing_weight, preferred_element_type=jnp.float32)
    ending_entries = settle(residual).astype(jnp.bfloat16)
    prediction_tensor = jnp.dot(ending_entries, cube_output_projector, preferred_element_type=jnp.float32).astype(jnp.bfloat16)
    return prediction_tensor.reshape(PRIOR_SNAPSHOTS, UNITS_WIDEWAYS // BLOCK_EDGE_UNITS, UNITS_DOWNWARD // BLOCK_EDGE_UNITS, UNITS_LENGTHWAYS // BLOCK_EDGE_UNITS, BLOCK_EDGE_UNITS ** 3)
```

```python
import functools
import math

import jax
import jax.numpy as jnp
import numpy as np
from jax import lax
from jax.experimental import pallas as pl
from jax.experimental.pallas import tpu as pltpu
from jax.sharding import PartitionSpec as P

CH = 16
D = 1024
HEADS = 8
HD = 128
EDGE = 8
TAPS = 3


def window_places():
    zin, yin = [], []
    for pair in range(3):
        zin += [2 * pair] * 8 + [2 * pair + 1] * 8
        yin += list(range(2, 10)) * 2
        zin += [2 * pair + o for o in (0, 0, 1, 1, 1, 1, 0, 0)]
        yin += [10, 11, 0, 1, 10, 11, 0, 1]
    return np.array(zin), np.array(yin)


def map_places():
    zin = [z for z in range(4) for _ in range(8)] + [z for z in range(4) for _ in range(2)]
    yin = [y + 1 for _ in range(4) for y in range(8)] + [0, 9] * 4
    return np.array(zin), np.array(yin)


def banded(row_z, row_y, col_z, col_y, taps):
    dz, dy = row_z - col_z, row_y - col_y
    total = 0.0
    for j in range(TAPS):
        for k in range(TAPS):
            total = total + jnp.where(jnp.asarray((dz == j) & (dy == k)), taps(j, k), 0.0)
    return total


def first_band(conv_first):
    group_z, group_y = map_places()
    row_z, row_y = window_places()
    col_z, col_y = np.repeat(group_z, CH), np.repeat(group_y, CH)
    taps = conv_first.reshape(CH, 27).T.astype(jnp.float32) * 0.5
    spread = jnp.tile(taps, (1, len(group_z))).reshape(3, 3, 3, 1, len(col_z))
    out = banded(row_z[:, None], row_y[:, None], col_z[None], col_y[None],
                 lambda j, k: spread[:, j, k])
    out = out.reshape(3 * len(row_z), -1)
    return jnp.pad(out, ((0, 256 - out.shape[0]), (0, 0))).astype(jnp.bfloat16)


def second_band(conv_second):
    group_z, group_y = map_places()
    col = np.arange(256)
    col_z, col_y = (col // 8) % 2, col % 8
    taps = conv_second.reshape(CH, CH, 27).transpose(2, 1, 0).astype(jnp.float32) * 0.5
    expand = jnp.asarray((col[None] // 16 == np.arange(CH)[:, None]).astype(np.float32), jnp.bfloat16)
    spread = jnp.dot(taps.reshape(-1, CH).astype(jnp.bfloat16), expand,
                     preferred_element_type=jnp.float32)
    spread = spread.reshape(3, 3, 3, 1, CH, 256)
    shape = (len(group_z), 1, 1)
    out = banded(group_z.reshape(shape), group_y.reshape(shape), col_z[None, None],
                 col_y[None, None], lambda j, k: spread[:, j, k])
    return out.reshape(3, len(group_z) * CH, 256).astype(jnp.bfloat16)


def edge_mask():
    p, zc, yc = np.arange(4), np.arange(2), np.arange(16)
    zin, side = np.arange(4), np.arange(2)
    p, _, zc, yc, zin, side, _ = np.meshgrid(
        p, np.arange(4), zc, yc, zin, side, np.arange(CH), indexing="ij")
    bad = (zin == 0) & (p == 0) & (zc == 0)
    bad |= (zin == 3) & (p == 3) & (zc == 1)
    bad |= (side == 0) & (yc == 0)
    bad |= (side == 1) & (yc == 15)
    return np.where(bad, 0.0, 1.0).reshape(512, 128)


def encode_kernel(place_ref, vol_ref, t1_ref, t2_ref, mask_ref, emb_ref, w_ref,
                  tok_ref, norm_ref, win_ref, maps_ref, acc_ref):
    step = pl.program_id(0)
    last = pl.num_programs(0) - 1

    @pl.when(step == 0)
    def _():
        acc_ref[...] = jnp.zeros_like(acc_ref)
        row = lax.broadcasted_iota(jnp.int32, (96, 128), 0) % 8
        lane = lax.broadcasted_iota(jnp.int32, (96, 128), 1)
        up_ok = (row >= 6) & (lane % 16 >= 1)
        down_ok = (row < 2) & (lane % 16 <= 14)
        zc = lax.broadcasted_iota(jnp.int32, (16, 128), 1) // 16 % 2

        @pl.loop(0, vol_ref.shape[0])
        def _(x):
            here = vol_ref[x].astype(jnp.float32)
            below = jnp.where(zc == 1, pltpu.roll(here[48:], 16, 1), 0.0)
            above = jnp.where(zc == 0, pltpu.roll(here[:16], 112, 1), 0.0)
            planes = jnp.concatenate([below, here, above], axis=0)
            halo = jnp.where(up_ok, pltpu.roll(planes, 1, 1), 0.0)
            halo = halo + jnp.where(down_ok, pltpu.roll(planes, 127, 1), 0.0)
            for q in range(6):
                win_ref[x, 24 * q:24 * q + 16] = planes[16 * q:16 * q + 16]
                win_ref[x, 24 * q + 16:24 * q + 24] = halo[16 * q:16 * q + 8] + pltpu.roll(
                    halo[16 * q + 8:16 * q + 16], 4, 0)

    slot = step % 3
    parts = []
    for p in range(4):
        rows = [win_ref[step + d, 24 * p:24 * p + 72] for d in range(3)]
        window = jnp.concatenate(rows + [jnp.zeros((40, 128), jnp.float32)], axis=0)
        parts.append(window.T.astype(jnp.bfloat16))
    window = jnp.concatenate(parts, axis=0)
    for lo, hi in ((0, 256), (256, 512), (512, 640)):
        half = jnp.dot(window, t1_ref[:, lo:hi], preferred_element_type=jnp.float32)
        maps = (half + half * jnp.tanh(half)).astype(jnp.bfloat16)
        if lo == 512:
            maps = maps * mask_ref[...]
        maps_ref[slot, :, lo:hi] = maps
    none = jnp.zeros((16, 128), jnp.bfloat16)
    for t in range(4):
        maps_ref[slot, 32 * t:32 * t + 16, 0:128] = none
        maps_ref[slot, 400 + 32 * t:416 + 32 * t, 384:512] = none

    outside = ((step == 0) & (place_ref[0] == 0)) | ((step == last) & (place_ref[0] == place_ref[1] - 1))

    @pl.when(outside)
    def _():
        maps_ref[slot] = jnp.zeros(maps_ref.shape[1:], jnp.bfloat16)

    @pl.when(step >= 2)
    def _():
        half = jnp.dot(maps_ref[(step + 1) % 3], t2_ref[0], preferred_element_type=jnp.float32)
        half += jnp.dot(maps_ref[(step + 2) % 3], t2_ref[1], preferred_element_type=jnp.float32)
        half += jnp.dot(maps_ref[slot], t2_ref[2], preferred_element_type=jnp.float32)
        second = (half + half * jnp.tanh(half)).astype(jnp.bfloat16)
        total = acc_ref[...]
        for p in range(4):
            weight = w_ref[:, 0, p].reshape(256, D)
            total += jnp.dot(second[128 * p:128 * p + 128], weight, preferred_element_type=jnp.float32)
        acc_ref[...] = total

    @pl.when(step == last)
    def _():
        tokens = (acc_ref[...] + emb_ref[...]).astype(jnp.bfloat16)
        tok_ref[...] = tokens
        wide = tokens.astype(jnp.float32)
        scale = lax.rsqrt(jnp.mean(wide * wide, axis=-1, keepdims=True) + 1e-05)
        norm_ref[...] = (wide * scale).astype(jnp.bfloat16)


def encode(place, volume_rows, t1, t2, mask, emb, patch_weight):
    planes = volume_rows.shape[0]
    whole = lambda shape: pl.BlockSpec(shape, lambda s: (0,) * len(shape))
    weight = patch_weight.reshape(CH, 8, 4, 16, D)
    return pl.pallas_call(
        encode_kernel,
        grid=(planes - 2,),
        in_specs=[
            pl.BlockSpec(memory_space=pltpu.SMEM),
            whole(volume_rows.shape), whole(t1.shape), whole(t2.shape), whole(mask.shape),
            whole(emb.shape),
            pl.BlockSpec((CH, 1, 4, 16, D), lambda s: (0, jnp.maximum(s - 2, 0), 0, 0, 0)),
        ],
        out_specs=[whole((128, D)), whole((128, D))],
        out_shape=[jax.ShapeDtypeStruct((128, D), jnp.bfloat16)] * 2,
        scratch_shapes=[
            pltpu.VMEM((planes, 144, 128), jnp.float32),
            pltpu.VMEM((3, 512, 640), jnp.bfloat16),
            pltpu.VMEM((128, D), jnp.float32),
        ],
        compiler_params=pltpu.CompilerParams(vmem_limit_bytes=40 * 2**20),
        cost_estimate=pl.CostEstimate(flops=8 * 10**9, bytes_accessed=20 * 2**20,
                                      transcendentals=5 * 10**6),
        name="encode",
    )(place, volume_rows, t1, t2, mask, emb, weight)


def settle(values_in):
    return values_in * lax.rsqrt(jnp.mean(values_in * values_in, axis=-1, keepdims=True) + 1e-05)


def embed_time(frame_index):
    frequency = jnp.exp(-math.log(1000.0) * jnp.arange(D, dtype=jnp.float32) / D)
    phase_shift = (jnp.arange(D) % 2).astype(jnp.float32) * (math.pi / 2)
    return (jnp.sin(frame_index.astype(jnp.float32)[:, None] * frequency + phase_shift), frequency)


def embed_space(tile_offset, place_x, place_z, place_y, frequency):
    along_x = (tile_offset[0] + EDGE * place_x).astype(jnp.float32)
    along_z = (tile_offset[1] + EDGE * place_z).astype(jnp.float32)
    along_y = (tile_offset[2] + EDGE * place_y).astype(jnp.float32)
    summed = jnp.sin(along_x[:, None, None, None] * frequency) + jnp.sin(
        along_z[None, :, None, None] * frequency + 1.0
    )
    summed = summed + jnp.sin(along_y[None, None, :, None] * frequency + 2.0)
    return summed.reshape(-1, D)


def attend_frames(query, keys_all, values_all, first_frame):
    cube_count = keys_all.shape[1]
    scores = jnp.einsum(
        "tnhd,smhd->htnsm", query, keys_all, preferred_element_type=jnp.float32
    ) / math.sqrt(HD)
    scores = scores.reshape(scores.shape[0], query.shape[0], query.shape[1], -1)
    query_frame = first_frame + jnp.arange(query.shape[0])
    allowed = jnp.arange(keys_all.shape[0])[None, :] <= query_frame[:, None]
    allowed = jnp.repeat(allowed, cube_count, axis=1)
    scores = jnp.where(allowed[None, :, None, :], scores, -1e30)
    shifted = jnp.exp(scores - jnp.max(scores, axis=-1, keepdims=True))
    weights = (shifted / jnp.sum(shifted, axis=-1, keepdims=True)).astype(jnp.bfloat16)
    flat_values = values_all.reshape(-1, values_all.shape[2], values_all.shape[3])
    return jnp.einsum(
        "htnk,khd->tnhd", weights, flat_values, preferred_element_type=jnp.float32
    ).astype(jnp.bfloat16)


def local(volume, frame_index, tile_offset, conv_first, conv_second, patch_weight,
          attend_weight, mixing_weight, cube_output_projector):
    frames, width, depth, height = volume.shape
    tile_place = lax.axis_index("tile")
    tiles = lax.axis_size("tile")
    rows = volume.reshape(frames, width, depth // 8, 8, height // 8, 8)
    rows = rows.transpose(1, 3, 5, 0, 2, 4).reshape(width, 64, 128)
    from_left = lax.ppermute(rows[-2:], "tile", [(i, i + 1) for i in range(tiles - 1)])
    from_right = lax.ppermute(rows[:2], "tile", [(i + 1, i) for i in range(tiles - 1)])
    volume_rows = jnp.concatenate([from_left, rows, from_right], axis=0)

    time_emb, frequency = embed_time(frame_index)
    space_emb = embed_space(tile_offset, tile_place + jnp.arange(1), jnp.arange(depth // EDGE),
                            jnp.arange(height // EDGE), frequency)
    emb = (time_emb[:, None, :] + space_emb[None]).reshape(-1, D)
    place = jnp.stack([tile_place, jnp.int32(tiles)]).astype(jnp.int32)
    token_rows, normed = encode(place, volume_rows, first_band(conv_first), second_band(conv_second),
                                jnp.asarray(edge_mask(), jnp.bfloat16), emb, patch_weight)

    row_count = token_rows.shape[0]
    projected = jnp.dot(normed, lax.all_gather(attend_weight, "tile", axis=1, tiled=True),
                        preferred_element_type=jnp.float32).astype(jnp.bfloat16)
    cube_count = row_count // frames
    projected = projected.reshape(frames, cube_count, 3, HEADS, HD)
    keys_values = lax.all_gather(projected[:, :, 1:], "tm", axis=0, tiled=True)
    attended = attend_frames(projected[:, :, 0], keys_values[:, :, 0], keys_values[:, :, 1],
                             lax.axis_index("tm") * frames)
    attended_rows = attended.reshape(row_count, D)
    mixed_terms = jnp.dot(attended_rows, lax.all_gather(mixing_weight, "tile", axis=1, tiled=True),
                          preferred_element_type=jnp.float32)
    residual = token_rows.astype(jnp.float32) + mixed_terms
    final_rows = settle(residual).astype(jnp.bfloat16)
    prediction = jnp.dot(final_rows, cube_output_projector,
                         preferred_element_type=jnp.float32).astype(jnp.bfloat16)
    return prediction.reshape(frames, width // EDGE, depth // EDGE, height // EDGE, -1)


def solution(mesh):
    placed = (P("tm", "tile", None, None), P("tm"), P(), P(), P(), P(), P(None, "tile"),
              P(None, "tile"), P())
    return jax.shard_map(local, mesh=mesh, in_specs=placed,
                         out_specs=P("tm", "tile", None, None, None), check_vma=False)
```

```python
import functools
import math

import jax
import jax.numpy as jnp
import numpy as np
from jax import lax
from jax.experimental import pallas as pl
from jax.experimental.pallas import tpu as pltpu
from jax.sharding import PartitionSpec as P

CH = 16
D = 1024
HEADS = 8
HD = 128
EDGE = 8
TAPS = 3


def window_places():
    zin, yin = [], []
    for pair in range(3):
        zin += [2 * pair] * 8 + [2 * pair + 1] * 8
        yin += list(range(2, 10)) * 2
        zin += [2 * pair + o for o in (0, 0, 1, 1, 1, 1, 0, 0)]
        yin += [10, 11, 0, 1, 10, 11, 0, 1]
    return np.array(zin), np.array(yin)


def map_places():
    zin = [z for z in range(4) for _ in range(8)] + [z for z in range(4) for _ in range(2)]
    yin = [y + 1 for _ in range(4) for y in range(8)] + [0, 9] * 4
    return np.array(zin), np.array(yin)


def banded(row_z, row_y, col_z, col_y, taps):
    dz, dy = row_z - col_z, row_y - col_y
    shared = (dz >= 0) & (dz < TAPS) & (dy >= 0) & (dy < TAPS)
    code = jnp.asarray(np.where(shared, dz * TAPS + dy, -1).astype(np.float32))
    total = 0.0
    for j in range(TAPS):
        for k in range(TAPS):
            total = total + jnp.where(code == float(j * TAPS + k), taps(j, k), 0.0)
    return total


def first_band(conv_first):
    group_z, group_y = map_places()
    row_z, row_y = window_places()
    col_z, col_y = np.repeat(group_z, CH), np.repeat(group_y, CH)
    taps = conv_first.reshape(CH, 27).T.astype(jnp.float32) * 0.5
    spread = jnp.tile(taps, (1, len(group_z))).reshape(3, 3, 3, 1, len(col_z))
    out = banded(row_z[:, None], row_y[:, None], col_z[None], col_y[None],
                 lambda j, k: spread[:, j, k])
    out = out.reshape(3 * len(row_z), -1)
    return jnp.pad(out, ((0, 256 - out.shape[0]), (0, 0))).astype(jnp.bfloat16)


def second_band(conv_second):
    group_z, group_y = map_places()
    col = np.arange(256)
    col_z, col_y = (col // 8) % 2, col % 8
    taps = conv_second.reshape(CH, CH, 27).transpose(2, 1, 0).astype(jnp.float32) * 0.5
    expand = jnp.asarray((col[None] // 16 == np.arange(CH)[:, None]).astype(np.float32), jnp.bfloat16)
    spread = jnp.dot(taps.reshape(-1, CH).astype(jnp.bfloat16), expand,
                     preferred_element_type=jnp.float32)
    spread = spread.reshape(3, 3, 3, 1, CH, 256)
    shape = (len(group_z), 1, 1)
    out = banded(group_z.reshape(shape), group_y.reshape(shape), col_z[None, None],
                 col_y[None, None], lambda j, k: spread[:, j, k])
    return out.reshape(3, len(group_z) * CH, 256).astype(jnp.bfloat16)


def edge_mask():
    p, zc, yc = np.arange(4), np.arange(2), np.arange(16)
    zin, side = np.arange(4), np.arange(2)
    p, _, zc, yc, zin, side, _ = np.meshgrid(
        p, np.arange(4), zc, yc, zin, side, np.arange(CH), indexing="ij")
    bad = (zin == 0) & (p == 0) & (zc == 0)
    bad |= (zin == 3) & (p == 3) & (zc == 1)
    bad |= (side == 0) & (yc == 0)
    bad |= (side == 1) & (yc == 15)
    return np.where(bad, 0.0, 1.0).reshape(512, 128)


def encode_kernel(place_ref, vol_ref, t1_ref, t2_ref, mask_ref, emb_ref, w_ref,
                  tok_ref, norm_ref, win_ref, maps_ref, acc_ref):
    step = pl.program_id(0)
    last = pl.num_programs(0) - 1

    @pl.when(step == 0)
    def _():
        acc_ref[...] = jnp.zeros_like(acc_ref)
        row = lax.broadcasted_iota(jnp.int32, (96, 128), 0) % 8
        lane = lax.broadcasted_iota(jnp.int32, (96, 128), 1)
        up_ok = (row >= 6) & (lane % 16 >= 1)
        down_ok = (row < 2) & (lane % 16 <= 14)
        zc = lax.broadcasted_iota(jnp.int32, (16, 128), 1) // 16 % 2

        @pl.loop(0, vol_ref.shape[0])
        def _(x):
            here = vol_ref[x].astype(jnp.float32)
            below = jnp.where(zc == 1, pltpu.roll(here[48:], 16, 1), 0.0)
            above = jnp.where(zc == 0, pltpu.roll(here[:16], 112, 1), 0.0)
            planes = jnp.concatenate([below, here, above], axis=0)
            halo = jnp.where(up_ok, pltpu.roll(planes, 1, 1), 0.0)
            halo = halo + jnp.where(down_ok, pltpu.roll(planes, 127, 1), 0.0)
            for q in range(6):
                win_ref[x, 24 * q:24 * q + 16] = planes[16 * q:16 * q + 16]
                win_ref[x, 24 * q + 16:24 * q + 24] = halo[16 * q:16 * q + 8] + pltpu.roll(
                    halo[16 * q + 8:16 * q + 16], 4, 0)

    slot = step % 3
    parts = []
    for p in range(4):
        rows = [win_ref[step + d, 24 * p:24 * p + 72] for d in range(3)]
        window = jnp.concatenate(rows + [jnp.zeros((40, 128), jnp.float32)], axis=0)
        parts.append(window.T.astype(jnp.bfloat16))
    window = jnp.concatenate(parts, axis=0)
    for lo, hi in ((0, 256), (256, 512), (512, 640)):
        half = jnp.dot(window, t1_ref[:, lo:hi], preferred_element_type=jnp.float32)
        maps = (half + half * jnp.tanh(half)).astype(jnp.bfloat16)
        if lo == 512:
            maps = maps * mask_ref[...]
        maps_ref[slot, :, lo:hi] = maps
    none = jnp.zeros((16, 128), jnp.bfloat16)
    for t in range(4):
        maps_ref[slot, 32 * t:32 * t + 16, 0:128] = none
        maps_ref[slot, 400 + 32 * t:416 + 32 * t, 384:512] = none

    outside = ((step == 0) & (place_ref[0] == 0)) | ((step == last) & (place_ref[0] == place_ref[1] - 1))

    @pl.when(outside)
    def _():
        maps_ref[slot] = jnp.zeros(maps_ref.shape[1:], jnp.bfloat16)

    @pl.when(step >= 2)
    def _():
        half = jnp.dot(maps_ref[(step + 1) % 3], t2_ref[0], preferred_element_type=jnp.float32)
        half += jnp.dot(maps_ref[(step + 2) % 3], t2_ref[1], preferred_element_type=jnp.float32)
        half += jnp.dot(maps_ref[slot], t2_ref[2], preferred_element_type=jnp.float32)
        second = (half + half * jnp.tanh(half)).astype(jnp.bfloat16)
        total = acc_ref[...]
        for p in range(4):
            weight = w_ref[:, 0, p].reshape(256, D)
            total += jnp.dot(second[128 * p:128 * p + 128], weight, preferred_element_type=jnp.float32)
        acc_ref[...] = total

    @pl.when(step == last)
    def _():
        tokens = (acc_ref[...] + emb_ref[...]).astype(jnp.bfloat16)
        tok_ref[...] = tokens
        wide = tokens.astype(jnp.float32)
        scale = lax.rsqrt(jnp.mean(wide * wide, axis=-1, keepdims=True) + 1e-05)
        norm_ref[...] = (wide * scale).astype(jnp.bfloat16)


def encode(place, volume_rows, t1, t2, mask, emb, patch_weight):
    planes = volume_rows.shape[0]
    whole = lambda shape: pl.BlockSpec(shape, lambda s: (0,) * len(shape))
    weight = patch_weight.reshape(CH, 8, 4, 16, D)
    return pl.pallas_call(
        encode_kernel,
        grid=(planes - 2,),
        in_specs=[
            pl.BlockSpec(memory_space=pltpu.SMEM),
            whole(volume_rows.shape), whole(t1.shape), whole(t2.shape), whole(mask.shape),
            whole(emb.shape),
            pl.BlockSpec((CH, 1, 4, 16, D), lambda s: (0, jnp.maximum(s - 2, 0), 0, 0, 0)),
        ],
        out_specs=[whole((128, D)), whole((128, D))],
        out_shape=[jax.ShapeDtypeStruct((128, D), jnp.bfloat16)] * 2,
        scratch_shapes=[
            pltpu.VMEM((planes, 144, 128), jnp.float32),
            pltpu.VMEM((3, 512, 640), jnp.bfloat16),
            pltpu.VMEM((128, D), jnp.float32),
        ],
        compiler_params=pltpu.CompilerParams(vmem_limit_bytes=40 * 2**20),
        cost_estimate=pl.CostEstimate(flops=8 * 10**9, bytes_accessed=20 * 2**20,
                                      transcendentals=5 * 10**6),
        name="encode",
    )(place, volume_rows, t1, t2, mask, emb, weight)


def settle(values_in):
    return values_in * lax.rsqrt(jnp.mean(values_in * values_in, axis=-1, keepdims=True) + 1e-05)


def embed_time(frame_index):
    frequency = jnp.exp(-math.log(1000.0) * jnp.arange(D, dtype=jnp.float32) / D)
    phase_shift = (jnp.arange(D) % 2).astype(jnp.float32) * (math.pi / 2)
    return (jnp.sin(frame_index.astype(jnp.float32)[:, None] * frequency + phase_shift), frequency)


def embed_space(tile_offset, place_x, place_z, place_y, frequency):
    along_x = (tile_offset[0] + EDGE * place_x).astype(jnp.float32)
    along_z = (tile_offset[1] + EDGE * place_z).astype(jnp.float32)
    along_y = (tile_offset[2] + EDGE * place_y).astype(jnp.float32)
    summed = jnp.sin(along_x[:, None, None, None] * frequency) + jnp.sin(
        along_z[None, :, None, None] * frequency + 1.0
    )
    summed = summed + jnp.sin(along_y[None, None, :, None] * frequency + 2.0)
    return summed.reshape(-1, D)


def partners():
    me = lax.axis_index("tm")
    sibling = me + 1 - 2 * (me % 2)
    return me, (sibling, (me + 2) % 4, (sibling + 2) % 4)


def attend_kernel(norm_ref, w0_ref, w1_ref, w2_ref, w3_ref, out_ref, rows_ref, qkv_ref, att_ref,
                  back_ref, send_sem, recv_sem, send_back, recv_back):
    me, others = partners()
    barrier = pltpu.get_barrier_semaphore()
    for other in others:
        pl.semaphore_signal(barrier, inc=1, device_id={"tm": other},
                            device_id_type=pl.DeviceIdType.MESH)
    pl.semaphore_wait(barrier, 3)
    sends = [
        pltpu.make_async_remote_copy(
            src_ref=norm_ref, dst_ref=rows_ref.at[me], send_sem=send_sem.at[i],
            recv_sem=recv_sem.at[i], device_id={"tm": other},
            device_id_type=pl.DeviceIdType.MESH)
        for i, other in enumerate(others)
    ]
    for send in sends:
        send.start()

    def project(block, source):
        total = jnp.zeros((128, 768), jnp.float32)
        for owner, w_ref in zip((me,) + others, (w0_ref, w1_ref, w2_ref, w3_ref)):
            part = source[:, pl.ds(pl.multiple_of(owner * 256, 256), 256)]
            total += jnp.dot(part, w_ref[...], preferred_element_type=jnp.float32)
        qkv_ref[block] = total.astype(jnp.bfloat16)

    project(me, norm_ref)
    for i, other in enumerate(others):
        sends[i].wait_recv()
        project(other, rows_ref.at[other])

    for head in range(2):
        lo = head * HD
        for block in range(4):
            query = qkv_ref[block, :, lo:lo + HD]
            count = 128 * (block + 1)
            keys = qkv_ref[:block + 1, :, 256 + lo:256 + lo + HD].reshape(count, HD)
            values = qkv_ref[:block + 1, :, 512 + lo:512 + lo + HD].reshape(count, HD)
            scores = lax.dot_general(query, keys, (((1,), (1,)), ((), ())),
                                     preferred_element_type=jnp.float32) / math.sqrt(HD)
            row = lax.broadcasted_iota(jnp.int32, (128, count), 0) // 32
            col = lax.broadcasted_iota(jnp.int32, (128, count), 1) // 32
            scores = jnp.where(col <= row + 4 * block, scores, -1e30)
            shifted = jnp.exp(scores - jnp.max(scores, axis=-1, keepdims=True))
            inverse = 1.0 / jnp.sum(shifted, axis=-1, keepdims=True)
            weights = (shifted * inverse).astype(jnp.bfloat16)
            att_ref[block, :, lo:lo + HD] = jnp.dot(
                weights, values, preferred_element_type=jnp.float32).astype(jnp.bfloat16)

    backs = [
        pltpu.make_async_remote_copy(
            src_ref=att_ref.at[other], dst_ref=back_ref.at[me], send_sem=send_back.at[i],
            recv_sem=recv_back.at[i], device_id={"tm": other},
            device_id_type=pl.DeviceIdType.MESH)
        for i, other in enumerate(others)
    ]
    for back in backs:
        back.start()
    out_ref[:, pl.ds(pl.multiple_of(me * 256, 256), 256)] = att_ref[me]
    for i, other in enumerate(others):
        backs[i].wait_recv()
        out_ref[:, pl.ds(pl.multiple_of(other * 256, 256), 256)] = back_ref[other]
    for i in range(3):
        sends[i].wait_send()
        backs[i].wait_send()


def attend(normed, weights):
    vmem = pl.BlockSpec(memory_space=pltpu.VMEM)
    return pl.pallas_call(
        attend_kernel,
        in_specs=[vmem] * 5,
        out_specs=vmem,
        out_shape=jax.ShapeDtypeStruct((128, D), jnp.bfloat16),
        scratch_shapes=[
            pltpu.VMEM((4, 128, D), jnp.bfloat16),
            pltpu.VMEM((4, 128, 768), jnp.bfloat16),
            pltpu.VMEM((4, 128, 256), jnp.bfloat16),
            pltpu.VMEM((4, 128, 256), jnp.bfloat16),
        ] + [pltpu.SemaphoreType.DMA((3,))] * 4,
        compiler_params=pltpu.CompilerParams(collective_id=0, has_side_effects=True,
                                             vmem_limit_bytes=32 * 2**20),
        cost_estimate=pl.CostEstimate(flops=10**9, bytes_accessed=2 * 2**20,
                                      transcendentals=4 * 10**5),
        name="attend",
    )(normed, *weights)


def head_weights(attend_weight):
    me = lax.axis_index("tm")
    quarter = lax.dynamic_slice_in_dim(attend_weight, me * 256, 256, axis=0)
    quarter = lax.all_gather(quarter, "tile", axis=1, tiled=True)

    def columns(member):
        return jnp.concatenate(
            [lax.dynamic_slice_in_dim(quarter, j * D + member * 256, 256, axis=1) for j in range(3)],
            axis=1)

    me, others = partners()
    pieces = [columns(me)]
    for i, other in enumerate(others):
        pieces.append(lax.ppermute(columns(other), "tm", [(m, m ^ (i + 1)) for m in range(4)]))
    return pieces


def local(volume, frame_index, tile_offset, conv_first, conv_second, patch_weight,
          attend_weight, mixing_weight, cube_output_projector):
    frames, width, depth, height = volume.shape
    tile_place = lax.axis_index("tile")
    tiles = lax.axis_size("tile")
    rows = volume.reshape(frames, width, depth // 8, 8, height // 8, 8)
    rows = rows.transpose(1, 3, 5, 0, 2, 4).reshape(width, 64, 128)
    from_left = lax.ppermute(rows[-2:], "tile", [(i, i + 1) for i in range(tiles - 1)])
    from_right = lax.ppermute(rows[:2], "tile", [(i + 1, i) for i in range(tiles - 1)])
    volume_rows = jnp.concatenate([from_left, rows, from_right], axis=0)

    time_emb, frequency = embed_time(frame_index)
    space_emb = embed_space(tile_offset, tile_place + jnp.arange(1), jnp.arange(depth // EDGE),
                            jnp.arange(height // EDGE), frequency)
    emb = (time_emb[:, None, :] + space_emb[None]).reshape(-1, D)
    place = jnp.stack([tile_place, jnp.int32(tiles)]).astype(jnp.int32)
    token_rows, normed = encode(place, volume_rows, first_band(conv_first), second_band(conv_second),
                                jnp.asarray(edge_mask(), jnp.bfloat16), emb, patch_weight)

    attended_rows = attend(normed, head_weights(attend_weight))
    mixed_terms = jnp.dot(attended_rows, lax.all_gather(mixing_weight, "tile", axis=1, tiled=True),
                          preferred_element_type=jnp.float32)
    residual = token_rows.astype(jnp.float32) + mixed_terms
    final_rows = settle(residual).astype(jnp.bfloat16)
    prediction = jnp.dot(final_rows, cube_output_projector,
                         preferred_element_type=jnp.float32).astype(jnp.bfloat16)
    return prediction.reshape(frames, width // EDGE, depth // EDGE, height // EDGE, -1)


def solution(mesh):
    placed = (P("tm", "tile", None, None), P("tm"), P(), P(), P(), P(), P(None, "tile"),
              P(None, "tile"), P())
    return jax.shard_map(local, mesh=mesh, in_specs=placed,
                         out_specs=P("tm", "tile", None, None, None), check_vma=False)
```

```python
import functools
import math

import jax
import jax.numpy as jnp
import numpy as np
from jax import lax
from jax.experimental import pallas as pl
from jax.experimental.pallas import tpu as pltpu
from jax.sharding import PartitionSpec as P

CH = 16
D = 1024
HEADS = 8
HD = 128
EDGE = 8
TAPS = 3


def window_places():
    zin, yin = [], []
    for pair in range(3):
        zin += [2 * pair] * 8 + [2 * pair + 1] * 8
        yin += list(range(2, 10)) * 2
        zin += [2 * pair + o for o in (0, 0, 1, 1, 1, 1, 0, 0)]
        yin += [10, 11, 0, 1, 10, 11, 0, 1]
    return np.array(zin), np.array(yin)


def map_places():
    zin = [z for z in range(4) for _ in range(8)] + [z for z in range(4) for _ in range(2)]
    yin = [y + 1 for _ in range(4) for y in range(8)] + [0, 9] * 4
    return np.array(zin), np.array(yin)


def banded(row_z, row_y, col_z, col_y, taps):
    dz, dy = row_z - col_z, row_y - col_y
    shared = (dz >= 0) & (dz < TAPS) & (dy >= 0) & (dy < TAPS)
    code = jnp.asarray(np.where(shared, dz * TAPS + dy, -1).astype(np.float32))
    total = 0.0
    for j in range(TAPS):
        for k in range(TAPS):
            total = total + jnp.where(code == float(j * TAPS + k), taps(j, k), 0.0)
    return total


def first_band(conv_first):
    group_z, group_y = map_places()
    row_z, row_y = window_places()
    col_z, col_y = np.repeat(group_z, CH), np.repeat(group_y, CH)
    taps = conv_first.reshape(CH, 27).T.astype(jnp.float32) * 0.5
    spread = jnp.tile(taps, (1, len(group_z))).reshape(3, 3, 3, 1, len(col_z))
    out = banded(row_z[:, None], row_y[:, None], col_z[None], col_y[None],
                 lambda j, k: spread[:, j, k])
    out = out.reshape(3 * len(row_z), -1)
    return jnp.pad(out, ((0, 256 - out.shape[0]), (0, 0))).astype(jnp.bfloat16)


def second_taps(conv_second):
    col = np.arange(256)
    taps = conv_second.reshape(CH, CH, 27).transpose(2, 1, 0)
    expand = jnp.asarray((col[None] // 16 == np.arange(CH)[:, None]).astype(np.float32) * 0.5, jnp.bfloat16)
    spread = jnp.dot(taps.reshape(-1, CH), expand, preferred_element_type=jnp.float32)
    return spread.reshape(27, CH, 256)


def second_code():
    group_z, group_y = map_places()
    col = np.arange(256)
    dz = group_z[:, None] - (col // 8 % 2)[None]
    dy = group_y[:, None] - (col % 8)[None]
    shared = (dz >= 0) & (dz < TAPS) & (dy >= 0) & (dy < TAPS)
    return np.where(shared, dz * TAPS + dy, -1).astype(np.float32).reshape(-1, 1, 256)


def edge_mask():
    p, zc, yc = np.arange(4), np.arange(2), np.arange(16)
    zin, side = np.arange(4), np.arange(2)
    p, _, zc, yc, zin, side, _ = np.meshgrid(
        p, np.arange(4), zc, yc, zin, side, np.arange(CH), indexing="ij")
    bad = (zin == 0) & (p == 0) & (zc == 0)
    bad |= (zin == 3) & (p == 3) & (zc == 1)
    bad |= (side == 0) & (yc == 0)
    bad |= (side == 1) & (yc == 15)
    return np.where(bad, 0.0, 1.0).reshape(512, 128)


def weight_place(unit):
    return pl.ds(pl.multiple_of((unit // HEADS) * 256 + (unit % 2) * HD, HD), HD)


def share_steps(step, last, attend_ref, own_ref, local_sem, send_sem, recv_sem):
    tile, member = lax.axis_index("tile"), lax.axis_index("tm")
    row, col = tile // 2, tile % 2
    beside = row * 2 + 1 - col
    column = [((row + d) % 4) * 2 + col for d in (1, 2, 3)]

    def wanted(unit):
        return (unit % HEADS) // 2 == member

    def remote(src, unit, kind, j, target):
        return pltpu.make_async_remote_copy(
            src_ref=src, dst_ref=own_ref.at[:, weight_place(unit)], send_sem=send_sem.at[kind, j],
            recv_sem=recv_sem.at[kind, j], device_id={"tile": target},
            device_id_type=pl.DeviceIdType.MESH)

    def own_copies(j):
        unit = tile * 3 + j
        src = attend_ref.at[:, j * HD:(j + 1) * HD]
        out = [remote(src, unit, 0, j, beside)]
        out += [remote(src, unit, d, j, column[d - 1]) for d in (1, 2, 3)]
        return out, pltpu.make_async_copy(src, own_ref.at[:, weight_place(unit)], local_sem.at[j])

    def passed_on(d, j):
        unit = (((row - d) % 4) * 2 + col) * 3 + j
        return unit, remote(own_ref.at[:, weight_place(unit)], unit, 3 + d, j, beside)

    @pl.when(step == 0)
    def _():
        barrier = pltpu.get_barrier_semaphore()
        for target in [beside] + column:
            pl.semaphore_signal(barrier, inc=1, device_id={"tile": target},
                                device_id_type=pl.DeviceIdType.MESH)
        pl.semaphore_wait(barrier, 4)
        for j in range(3):
            @pl.when(wanted(tile * 3 + j))
            def _():
                copies, here = own_copies(j)
                for copy in copies:
                    copy.start()
                here.start()

    for d, when in ((1, 4), (3, 5), (2, 6)):
        @pl.when(step == when)
        def _():
            for j in range(3):
                unit, onward = passed_on(d, j)

                @pl.when(wanted(unit))
                def _():
                    remote(attend_ref.at[:, j * HD:(j + 1) * HD], unit, d, j, beside).wait_recv()
                    onward.start()

    @pl.when(step == last)
    def _():
        for j in range(3):
            @pl.when(wanted(tile * 3 + j))
            def _():
                copies, here = own_copies(j)
                for copy in copies:
                    copy.wait_send()
                here.wait()

            for d in (1, 2, 3):
                unit, onward = passed_on(d, j)

                @pl.when(wanted(unit))
                def _():
                    onward.wait_send()

            for kind, back in ((0, 0), (4, 1), (5, 2), (6, 3)):
                unit = (((row - back) % 4) * 2 + 1 - col) * 3 + j

                @pl.when(wanted(unit))
                def _():
                    remote(attend_ref.at[:, j * HD:(j + 1) * HD], unit, kind, j, beside).wait_recv()


def encode_kernel(share, *refs):
    vol_ref, t1_ref, taps_ref, code_ref, mask_ref, emb_ref, w_ref = refs[:7]
    if share:
        attend_ref, tok_ref, norm_ref, own_ref = refs[7:11]
        win_ref, maps_ref, acc_ref, t2_ref = refs[11:15]
    else:
        tok_ref, norm_ref, win_ref, maps_ref, acc_ref, t2_ref = refs[7:]
    step = pl.program_id(0)
    last = pl.num_programs(0) - 1
    if share:
        share_steps(step, last, attend_ref, own_ref, *refs[15:])

    @pl.when(step == 0)
    def _():
        acc_ref[...] = jnp.zeros_like(acc_ref)

        @pl.loop(0, code_ref.shape[0])
        def _(group):
            code = code_ref[group]
            for dx in range(3):
                total = jnp.zeros((CH, 256), jnp.float32)
                for tap in range(9):
                    total += jnp.where(code == float(tap), taps_ref[9 * dx + tap], 0.0)
                t2_ref[dx, pl.ds(pl.multiple_of(group * CH, CH), CH)] = total.astype(jnp.bfloat16)

        row = lax.broadcasted_iota(jnp.int32, (96, 128), 0) % 8
        lane = lax.broadcasted_iota(jnp.int32, (96, 128), 1)
        up_ok = (row >= 6) & (lane % 16 >= 1)
        down_ok = (row < 2) & (lane % 16 <= 14)
        zc = lax.broadcasted_iota(jnp.int32, (16, 128), 1) // 16 % 2

        @pl.loop(0, vol_ref.shape[0])
        def _(x):
            here = vol_ref[x].astype(jnp.float32)
            below = jnp.where(zc == 1, pltpu.roll(here[48:], 16, 1), 0.0)
            above = jnp.where(zc == 0, pltpu.roll(here[:16], 112, 1), 0.0)
            planes = jnp.concatenate([below, here, above], axis=0)
            halo = jnp.where(up_ok, pltpu.roll(planes, 1, 1), 0.0)
            halo = halo + jnp.where(down_ok, pltpu.roll(planes, 127, 1), 0.0)
            for q in range(6):
                win_ref[x, 24 * q:24 * q + 16] = planes[16 * q:16 * q + 16]
                win_ref[x, 24 * q + 16:24 * q + 24] = halo[16 * q:16 * q + 8] + pltpu.roll(
                    halo[16 * q + 8:16 * q + 16], 4, 0)

    slot = step % 3
    parts = []
    for p in range(4):
        rows = [win_ref[step + d, 24 * p:24 * p + 72] for d in range(3)]
        window = jnp.concatenate(rows + [jnp.zeros((40, 128), jnp.float32)], axis=0)
        parts.append(window.T.astype(jnp.bfloat16))
    window = jnp.concatenate(parts, axis=0)
    for lo, hi in ((0, 256), (256, 512), (512, 640)):
        half = jnp.dot(window, t1_ref[:, lo:hi], preferred_element_type=jnp.float32)
        maps = (half + half * jnp.tanh(half)).astype(jnp.bfloat16)
        if lo == 512:
            maps = maps * mask_ref[...]
        maps_ref[slot, :, lo:hi] = maps
    none = jnp.zeros((16, 128), jnp.bfloat16)
    for t in range(4):
        maps_ref[slot, 32 * t:32 * t + 16, 0:128] = none
        maps_ref[slot, 400 + 32 * t:416 + 32 * t, 384:512] = none

    tile = lax.axis_index("tile")
    outside = ((step == 0) & (tile == 0)) | ((step == last) & (tile == lax.axis_size("tile") - 1))

    @pl.when(outside)
    def _():
        maps_ref[slot] = jnp.zeros(maps_ref.shape[1:], jnp.bfloat16)

    @pl.when(step >= 2)
    def _():
        half = jnp.dot(maps_ref[(step + 1) % 3], t2_ref[0], preferred_element_type=jnp.float32)
        half += jnp.dot(maps_ref[(step + 2) % 3], t2_ref[1], preferred_element_type=jnp.float32)
        half += jnp.dot(maps_ref[slot], t2_ref[2], preferred_element_type=jnp.float32)
        second = (half + half * jnp.tanh(half)).astype(jnp.bfloat16)
        total = acc_ref[...]
        for p in range(4):
            weight = w_ref[:, 0, p].reshape(256, D)
            total += jnp.dot(second[128 * p:128 * p + 128], weight, preferred_element_type=jnp.float32)
        acc_ref[...] = total

    @pl.when(step == last)
    def _():
        tokens = (acc_ref[...] + emb_ref[...]).astype(jnp.bfloat16)
        tok_ref[...] = tokens
        wide = tokens.astype(jnp.float32)
        scale = lax.rsqrt(jnp.mean(wide * wide, axis=-1, keepdims=True) + 1e-05)
        norm_ref[...] = (wide * scale).astype(jnp.bfloat16)


def encode(volume_rows, t1, taps, emb, patch_weight, attend_weight):
    planes = volume_rows.shape[0]
    share = attend_weight is not None
    whole = lambda shape: pl.BlockSpec(shape, lambda s: (0,) * len(shape))
    weight = patch_weight.reshape(CH, 8, 4, 16, D)
    code, mask = jnp.asarray(second_code()), jnp.asarray(edge_mask(), jnp.bfloat16)
    held = [volume_rows, t1, taps, code, mask, emb]
    in_specs = [whole(array.shape) for array in held]
    in_specs.append(pl.BlockSpec((CH, 1, 4, 16, D), lambda s: (0, jnp.maximum(s - 2, 0), 0, 0, 0)))
    out_specs = [whole((128, D)), whole((128, D))]
    out_shape = [jax.ShapeDtypeStruct((128, D), jnp.bfloat16)] * 2
    scratch = [
        pltpu.VMEM((planes, 144, 128), jnp.float32),
        pltpu.VMEM((3, 512, 640), jnp.bfloat16),
        pltpu.VMEM((128, D), jnp.float32),
        pltpu.VMEM((3, 640, 256), jnp.bfloat16),
    ]
    operands = held + [weight]
    extra = {}
    if share:
        operands.append(attend_weight)
        in_specs.append(pl.BlockSpec(memory_space=pl.ANY))
        out_specs.append(pl.BlockSpec(memory_space=pl.ANY))
        out_shape.append(jax.ShapeDtypeStruct((D, 768), jnp.bfloat16))
        scratch += [pltpu.SemaphoreType.DMA((3,)), pltpu.SemaphoreType.DMA((7, 3)),
                    pltpu.SemaphoreType.DMA((7, 3))]
        extra = dict(collective_id=1, has_side_effects=True)
    return pl.pallas_call(
        functools.partial(encode_kernel, share),
        grid=(planes - 2,),
        in_specs=in_specs,
        out_specs=out_specs,
        out_shape=out_shape,
        scratch_shapes=scratch,
        compiler_params=pltpu.CompilerParams(vmem_limit_bytes=40 * 2**20, **extra),
        cost_estimate=pl.CostEstimate(flops=8 * 10**9, bytes_accessed=20 * 2**20,
                                      transcendentals=5 * 10**6),
        name="encode",
    )(*operands)


def settle(values_in):
    return values_in * lax.rsqrt(jnp.mean(values_in * values_in, axis=-1, keepdims=True) + 1e-05)


def embed_time(frame_index):
    frequency = jnp.exp(-math.log(1000.0) * jnp.arange(D, dtype=jnp.float32) / D)
    phase_shift = (jnp.arange(D) % 2).astype(jnp.float32) * (math.pi / 2)
    return (jnp.sin(frame_index.astype(jnp.float32)[:, None] * frequency + phase_shift), frequency)


def embed_space(tile_offset, place_x, place_z, place_y, frequency):
    along_x = (tile_offset[0] + EDGE * place_x).astype(jnp.float32)
    along_z = (tile_offset[1] + EDGE * place_z).astype(jnp.float32)
    along_y = (tile_offset[2] + EDGE * place_y).astype(jnp.float32)
    summed = jnp.sin(along_x[:, None, None, None] * frequency) + jnp.sin(
        along_z[None, :, None, None] * frequency + 1.0
    )
    summed = summed + jnp.sin(along_y[None, None, :, None] * frequency + 2.0)
    return summed.reshape(-1, D)


def partners():
    me = lax.axis_index("tm")
    sibling = me + 1 - 2 * (me % 2)
    return me, (sibling, (me + 2) % 4, (sibling + 2) % 4)


def attend_kernel(norm_ref, w_ref, out_ref, rows_ref, qkv_ref, att_ref,
                  back_ref, send_sem, recv_sem, send_back, recv_back):
    me, others = partners()
    barrier = pltpu.get_barrier_semaphore()
    for other in others:
        pl.semaphore_signal(barrier, inc=1, device_id={"tm": other},
                            device_id_type=pl.DeviceIdType.MESH)
    pl.semaphore_wait(barrier, 3)
    sends = [
        pltpu.make_async_remote_copy(
            src_ref=norm_ref, dst_ref=rows_ref.at[me], send_sem=send_sem.at[i],
            recv_sem=recv_sem.at[i], device_id={"tm": other},
            device_id_type=pl.DeviceIdType.MESH)
        for i, other in enumerate(others)
    ]
    for send in sends:
        send.start()

    def project(block, source):
        total = jnp.dot(source[...], w_ref[...], preferred_element_type=jnp.float32)
        qkv_ref[block] = total.astype(jnp.bfloat16)

    project(me, norm_ref)
    for i, other in enumerate(others):
        sends[i].wait_recv()
        project(other, rows_ref.at[other])

    for head in range(2):
        lo = head * HD
        for block in range(4):
            query = qkv_ref[block, :, lo:lo + HD]
            count = 128 * (block + 1)
            keys = qkv_ref[:block + 1, :, 256 + lo:256 + lo + HD].reshape(count, HD)
            values = qkv_ref[:block + 1, :, 512 + lo:512 + lo + HD].reshape(count, HD)
            scores = lax.dot_general(query, keys, (((1,), (1,)), ((), ())),
                                     preferred_element_type=jnp.float32) / math.sqrt(HD)
            row = lax.broadcasted_iota(jnp.int32, (128, count), 0) // 32
            col = lax.broadcasted_iota(jnp.int32, (128, count), 1) // 32
            scores = jnp.where(col <= row + 4 * block, scores, -1e30)
            shifted = jnp.exp(scores - jnp.max(scores, axis=-1, keepdims=True))
            inverse = 1.0 / jnp.sum(shifted, axis=-1, keepdims=True)
            weights = (shifted * inverse).astype(jnp.bfloat16)
            att_ref[block, :, lo:lo + HD] = jnp.dot(
                weights, values, preferred_element_type=jnp.float32).astype(jnp.bfloat16)

    backs = [
        pltpu.make_async_remote_copy(
            src_ref=att_ref.at[other], dst_ref=back_ref.at[me], send_sem=send_back.at[i],
            recv_sem=recv_back.at[i], device_id={"tm": other},
            device_id_type=pl.DeviceIdType.MESH)
        for i, other in enumerate(others)
    ]
    for back in backs:
        back.start()
    out_ref[:, pl.ds(pl.multiple_of(me * 256, 256), 256)] = att_ref[me]
    for i, other in enumerate(others):
        backs[i].wait_recv()
        out_ref[:, pl.ds(pl.multiple_of(other * 256, 256), 256)] = back_ref[other]
    for i in range(3):
        sends[i].wait_send()
        backs[i].wait_send()


def attend(normed, weights):
    vmem = pl.BlockSpec(memory_space=pltpu.VMEM)
    return pl.pallas_call(
        attend_kernel,
        in_specs=[vmem] * 2,
        out_specs=vmem,
        out_shape=jax.ShapeDtypeStruct((128, D), jnp.bfloat16),
        scratch_shapes=[
            pltpu.VMEM((4, 128, D), jnp.bfloat16),
            pltpu.VMEM((4, 128, 768), jnp.bfloat16),
            pltpu.VMEM((4, 128, 256), jnp.bfloat16),
            pltpu.VMEM((4, 128, 256), jnp.bfloat16),
        ] + [pltpu.SemaphoreType.DMA((3,))] * 4,
        compiler_params=pltpu.CompilerParams(collective_id=0, has_side_effects=True,
                                             vmem_limit_bytes=32 * 2**20),
        cost_estimate=pl.CostEstimate(flops=10**9, bytes_accessed=2 * 2**20,
                                      transcendentals=4 * 10**5),
        name="attend",
    )(normed, weights)


def head_weights(attend_weight):
    me = lax.axis_index("tm")
    quarter = lax.dynamic_slice_in_dim(attend_weight, me * 256, 256, axis=0)
    quarter = lax.all_gather(quarter, "tile", axis=1, tiled=True)

    def columns(member):
        return jnp.concatenate(
            [lax.dynamic_slice_in_dim(quarter, j * D + member * 256, 256, axis=1) for j in range(3)],
            axis=1)

    me, others = partners()
    weights = jnp.zeros((D, 768), attend_weight.dtype)
    weights = lax.dynamic_update_slice_in_dim(weights, columns(me), me * 256, axis=0)
    for i, other in enumerate(others):
        piece = lax.ppermute(columns(other), "tm", [(m, m ^ (i + 1)) for m in range(4)])
        weights = lax.dynamic_update_slice_in_dim(weights, piece, other * 256, axis=0)
    return weights


def local(volume, frame_index, tile_offset, conv_first, conv_second, patch_weight,
          attend_weight, mixing_weight, cube_output_projector):
    frames, width, depth, height = volume.shape
    tile_place = lax.axis_index("tile")
    tiles = lax.axis_size("tile")
    rows = volume.reshape(frames, width, depth // 8, 8, height // 8, 8)
    rows = rows.transpose(1, 3, 5, 0, 2, 4).reshape(width, 64, 128)
    from_left = lax.ppermute(rows[-2:], "tile", [(i, i + 1) for i in range(tiles - 1)])
    from_right = lax.ppermute(rows[:2], "tile", [(i + 1, i) for i in range(tiles - 1)])
    volume_rows = jnp.concatenate([from_left, rows, from_right], axis=0)

    time_emb, frequency = embed_time(frame_index)
    space_emb = embed_space(tile_offset, tile_place + jnp.arange(1), jnp.arange(depth // EDGE),
                            jnp.arange(height // EDGE), frequency)
    emb = (time_emb[:, None, :] + space_emb[None]).reshape(-1, D)
    t1, taps = first_band(conv_first), second_taps(conv_second)
    if tiles == 8 and attend_weight.shape[1] == 3 * HD:
        token_rows, normed, weights = encode(volume_rows, t1, taps, emb, patch_weight, attend_weight)
    else:
        token_rows, normed = encode(volume_rows, t1, taps, emb, patch_weight, None)
        weights = head_weights(attend_weight)
    attended_rows = attend(normed, weights)
    mixed_terms = jnp.dot(attended_rows, lax.all_gather(mixing_weight, "tile", axis=1, tiled=True),
                          preferred_element_type=jnp.float32)
    residual = token_rows.astype(jnp.float32) + mixed_terms
    final_rows = settle(residual).astype(jnp.bfloat16)
    prediction = jnp.dot(final_rows, cube_output_projector,
                         preferred_element_type=jnp.float32).astype(jnp.bfloat16)
    return prediction.reshape(frames, width // EDGE, depth // EDGE, height // EDGE, -1)


def solution(mesh):
    placed = (P("tm", "tile", None, None), P("tm"), P(), P(), P(), P(), P(None, "tile"),
              P(None, "tile"), P())
    return jax.shard_map(local, mesh=mesh, in_specs=placed,
                         out_specs=P("tm", "tile", None, None, None), check_vma=False)
```

```python
import functools
import math

import jax
import jax.numpy as jnp
import numpy as np
from jax import lax
from jax.experimental import pallas as pl
from jax.experimental.pallas import tpu as pltpu
from jax.sharding import PartitionSpec as P

CH = 16
D = 1024
HEADS = 8
HD = 128
EDGE = 8
TAPS = 3


def window_places():
    zin, yin = [], []
    for pair in range(3):
        zin += [2 * pair] * 8 + [2 * pair + 1] * 8
        yin += list(range(2, 10)) * 2
        zin += [2 * pair + o for o in (0, 0, 1, 1, 1, 1, 0, 0)]
        yin += [10, 11, 0, 1, 10, 11, 0, 1]
    return np.array(zin), np.array(yin)


def map_places():
    zin = [z for z in range(4) for _ in range(8)] + [z for z in range(4) for _ in range(2)]
    yin = [y + 1 for _ in range(4) for y in range(8)] + [0, 9] * 4
    return np.array(zin), np.array(yin)


def banded(row_z, row_y, col_z, col_y, taps):
    dz, dy = row_z - col_z, row_y - col_y
    shared = (dz >= 0) & (dz < TAPS) & (dy >= 0) & (dy < TAPS)
    code = jnp.asarray(np.where(shared, dz * TAPS + dy, -1).astype(np.float32))
    total = 0.0
    for j in range(TAPS):
        for k in range(TAPS):
            total = total + jnp.where(code == float(j * TAPS + k), taps(j, k), 0.0)
    return total


def first_band(conv_first):
    group_z, group_y = map_places()
    row_z, row_y = window_places()
    col_z, col_y = np.repeat(group_z, CH), np.repeat(group_y, CH)
    taps = conv_first.reshape(CH, 27).T.astype(jnp.float32) * 0.5
    spread = jnp.tile(taps, (1, len(group_z))).reshape(3, 3, 3, 1, len(col_z))
    out = banded(row_z[:, None], row_y[:, None], col_z[None], col_y[None],
                 lambda j, k: spread[:, j, k])
    out = out.reshape(3 * len(row_z), -1)
    return jnp.pad(out, ((0, 256 - out.shape[0]), (0, 0))).astype(jnp.bfloat16)


def second_taps(conv_second):
    col = np.arange(256)
    taps = conv_second.transpose(2, 3, 4, 0, 1).reshape(27, CH, CH)
    expand = jnp.asarray((col[None] // 16 == np.arange(CH)[:, None]).astype(np.float32) * 0.5, jnp.bfloat16)
    spread = lax.dot_general(taps, expand, (((1,), (0,)), ((), ())), preferred_element_type=jnp.float32)
    return spread.reshape(27, CH, 256)


def second_code():
    group_z, group_y = map_places()
    col = np.arange(256)
    dz = group_z[:, None] - (col // 8 % 2)[None]
    dy = group_y[:, None] - (col % 8)[None]
    shared = (dz >= 0) & (dz < TAPS) & (dy >= 0) & (dy < TAPS)
    return np.where(shared, dz * TAPS + dy, -1).astype(np.float32).reshape(-1, 1, 256)


def edge_mask():
    p, zc, yc = np.arange(4), np.arange(2), np.arange(16)
    zin, side = np.arange(4), np.arange(2)
    p, _, zc, yc, zin, side, _ = np.meshgrid(
        p, np.arange(4), zc, yc, zin, side, np.arange(CH), indexing="ij")
    bad = (zin == 0) & (p == 0) & (zc == 0)
    bad |= (zin == 3) & (p == 3) & (zc == 1)
    bad |= (side == 0) & (yc == 0)
    bad |= (side == 1) & (yc == 15)
    return np.where(bad, 0.0, 1.0).reshape(512, 128)


def share_steps(step, last, vol_ref, attend_ref, mixing_ref, own_ref, mix_ref, halo_ref, halo_send,
                halo_recv, local_sem, send_sem, recv_sem):
    tile, member = lax.axis_index("tile"), lax.axis_index("tm")
    ends = lax.axis_size("tile") - 1
    row, col = tile // 2, tile % 2
    beside = row * 2 + 1 - col
    column = [((row + d) % 4) * 2 + col for d in (1, 2, 3)]
    far = tile - 1 + 2 * col
    has_far = ((col == 0) & (tile > 0)) | ((col == 1) & (tile < ends))
    mine = pl.ds(pl.multiple_of(member * 256, 256), 256)

    def wanted(owner, j):
        return ((owner * 3 + j) % HEADS) // 2 == member if j < 3 else member >= 0

    def block(owner, j):
        if j == 3:
            return mix_ref.at[owner]
        unit = owner * 3 + j
        return own_ref.at[(unit // HEADS) * 2 + unit % 2]

    def source(j):
        return mixing_ref.at[mine] if j == 3 else attend_ref.at[:, j * HD:(j + 1) * HD]

    def remote(src, owner, kind, j, target):
        return pltpu.make_async_remote_copy(
            src_ref=src, dst_ref=block(owner, j), send_sem=send_sem.at[kind, j],
            recv_sem=recv_sem.at[kind, j], device_id={"tile": target},
            device_id_type=pl.DeviceIdType.MESH)

    def own_copies(j):
        out = [remote(source(j), tile, d, j, column[d - 1]) for d in (1, 2, 3)]
        out.append(remote(source(j), tile, 0, j, beside))
        return out, pltpu.make_async_copy(source(j), block(tile, j), local_sem.at[j])

    def passed_on(d, j):
        owner = ((row - d) % 4) * 2 + col
        return owner, remote(block(owner, j), owner, 3 + d, j, beside)

    def halo(side, target):
        src = vol_ref.at[vol_ref.shape[0] - 2:] if side == 0 else vol_ref.at[:2]
        return pltpu.make_async_remote_copy(
            src_ref=src, dst_ref=halo_ref.at[side], send_sem=halo_send.at[side],
            recv_sem=halo_recv.at[side], device_id={"tile": target},
            device_id_type=pl.DeviceIdType.MESH)

    @pl.when(step == 0)
    def _():
        barrier = pltpu.get_barrier_semaphore()
        for target in [beside] + column:
            pl.semaphore_signal(barrier, inc=1, device_id={"tile": target},
                                device_id_type=pl.DeviceIdType.MESH)

        @pl.when(has_far)
        def _():
            pl.semaphore_signal(barrier, inc=1, device_id={"tile": far},
                                device_id_type=pl.DeviceIdType.MESH)
            pl.semaphore_wait(barrier, 5)

        @pl.when(jnp.logical_not(has_far))
        def _():
            pl.semaphore_wait(barrier, 4)

        @pl.when(tile < ends)
        def _():
            halo(0, tile + 1).start()

        @pl.when(tile > 0)
        def _():
            halo(1, tile - 1).start()

        for j in range(4):
            @pl.when(wanted(tile, j))
            def _():
                copies, here = own_copies(j)
                for copy in copies:
                    copy.start()
                here.start()

        @pl.when(tile > 0)
        def _():
            halo(0, tile - 1).wait_recv()

        @pl.when(tile == 0)
        def _():
            halo_ref[0] = jnp.zeros(halo_ref.shape[1:], halo_ref.dtype)

        @pl.when(tile < ends)
        def _():
            halo(1, tile + 1).wait_recv()

        @pl.when(tile == ends)
        def _():
            halo_ref[1] = jnp.zeros(halo_ref.shape[1:], halo_ref.dtype)

    for d, when in ((1, 4), (3, 5), (2, 6)):
        @pl.when(step == when)
        def _():
            for j in range(4):
                owner, onward = passed_on(d, j)

                @pl.when(wanted(owner, j))
                def _():
                    remote(source(j), owner, d, j, beside).wait_recv()
                    onward.start()

    @pl.when(step == last)
    def _():
        @pl.when(tile < ends)
        def _():
            halo(0, tile + 1).wait_send()

        @pl.when(tile > 0)
        def _():
            halo(1, tile - 1).wait_send()

        for j in range(4):
            @pl.when(wanted(tile, j))
            def _():
                copies, here = own_copies(j)
                for copy in copies:
                    copy.wait_send()
                here.wait()

            for d in (1, 2, 3):
                owner, onward = passed_on(d, j)

                @pl.when(wanted(owner, j))
                def _():
                    onward.wait_send()

            for kind, back in ((0, 0), (4, 1), (5, 2), (6, 3)):
                owner = ((row - back) % 4) * 2 + 1 - col

                @pl.when(wanted(owner, j))
                def _():
                    remote(source(j), owner, kind, j, beside).wait_recv()


def encode_kernel(share, *refs):
    vol_ref, t1_ref, taps_ref, code_ref, mask_ref, emb_ref, w_ref = refs[:7]
    if share:
        attend_ref, mixing_ref, tok_ref, norm_ref, own_ref, mix_ref = refs[7:13]
        win_ref, maps_ref, acc_ref, t2_ref, halo_ref = refs[13:18]
    else:
        tok_ref, norm_ref, win_ref, maps_ref, acc_ref, t2_ref = refs[7:]
    step = pl.program_id(0)
    last = pl.num_programs(0) - 1
    if share:
        share_steps(step, last, vol_ref, attend_ref, mixing_ref, own_ref, mix_ref, halo_ref, *refs[18:])

    @pl.when(step == 0)
    def _():
        acc_ref[...] = jnp.zeros_like(acc_ref)

        @pl.loop(0, code_ref.shape[0])
        def _(group):
            code = code_ref[group]
            for dx in range(3):
                total = jnp.zeros((CH, 256), jnp.float32)
                for tap in range(9):
                    total += jnp.where(code == float(tap), taps_ref[9 * dx + tap], 0.0)
                t2_ref[dx, pl.ds(pl.multiple_of(group * CH, CH), CH)] = total.astype(jnp.bfloat16)

        row = lax.broadcasted_iota(jnp.int32, (96, 128), 0) % 8
        lane = lax.broadcasted_iota(jnp.int32, (96, 128), 1)
        up_ok = (row >= 6) & (lane % 16 >= 1)
        down_ok = (row < 2) & (lane % 16 <= 14)
        zc = lax.broadcasted_iota(jnp.int32, (16, 128), 1) // 16 % 2

        def window_plane(x, plane):
            here = plane.astype(jnp.float32)
            below = jnp.where(zc == 1, pltpu.roll(here[48:], 16, 1), 0.0)
            above = jnp.where(zc == 0, pltpu.roll(here[:16], 112, 1), 0.0)
            planes = jnp.concatenate([below, here, above], axis=0)
            halo = jnp.where(up_ok, pltpu.roll(planes, 1, 1), 0.0)
            halo = halo + jnp.where(down_ok, pltpu.roll(planes, 127, 1), 0.0)
            for q in range(6):
                win_ref[x, 24 * q:24 * q + 16] = planes[16 * q:16 * q + 16]
                win_ref[x, 24 * q + 16:24 * q + 24] = halo[16 * q:16 * q + 8] + pltpu.roll(
                    halo[16 * q + 8:16 * q + 16], 4, 0)

        @pl.loop(0, vol_ref.shape[0])
        def _(x):
            window_plane(x + (2 if share else 0), vol_ref[x])

        if share:
            @pl.loop(0, 2)
            def _(x):
                window_plane(x, halo_ref[0, x])
                window_plane(vol_ref.shape[0] + 2 + x, halo_ref[1, x])

    slot = step % 3
    parts = []
    for p in range(4):
        rows = [win_ref[step + d, 24 * p:24 * p + 72] for d in range(3)]
        window = jnp.concatenate(rows + [jnp.zeros((40, 128), jnp.float32)], axis=0)
        parts.append(window.T.astype(jnp.bfloat16))
    window = jnp.concatenate(parts, axis=0)
    for lo, hi in ((0, 256), (256, 512), (512, 640)):
        half = jnp.dot(window, t1_ref[:, lo:hi], preferred_element_type=jnp.float32)
        maps = (half + half * jnp.tanh(half)).astype(jnp.bfloat16)
        if lo == 512:
            maps = maps * mask_ref[...]
        maps_ref[slot, :, lo:hi] = maps
    none = jnp.zeros((16, 128), jnp.bfloat16)
    for t in range(4):
        maps_ref[slot, 32 * t:32 * t + 16, 0:128] = none
        maps_ref[slot, 400 + 32 * t:416 + 32 * t, 384:512] = none

    tile = lax.axis_index("tile")
    outside = ((step == 0) & (tile == 0)) | ((step == last) & (tile == lax.axis_size("tile") - 1))

    @pl.when(outside)
    def _():
        maps_ref[slot] = jnp.zeros(maps_ref.shape[1:], jnp.bfloat16)

    @pl.when(step >= 2)
    def _():
        half = jnp.dot(maps_ref[(step + 1) % 3], t2_ref[0], preferred_element_type=jnp.float32)
        half += jnp.dot(maps_ref[(step + 2) % 3], t2_ref[1], preferred_element_type=jnp.float32)
        half += jnp.dot(maps_ref[slot], t2_ref[2], preferred_element_type=jnp.float32)
        second = (half + half * jnp.tanh(half)).astype(jnp.bfloat16)
        total = acc_ref[...]
        for p in range(4):
            weight = w_ref[:, 0, p].reshape(256, D)
            total += jnp.dot(second[128 * p:128 * p + 128], weight, preferred_element_type=jnp.float32)
        acc_ref[...] = total

    @pl.when(step == last)
    def _():
        tokens = (acc_ref[...] + emb_ref[...]).astype(jnp.bfloat16)
        tok_ref[...] = tokens
        wide = tokens.astype(jnp.float32)
        scale = lax.rsqrt(jnp.mean(wide * wide, axis=-1, keepdims=True) + 1e-05)
        norm_ref[...] = (wide * scale).astype(jnp.bfloat16)


def encode(volume_rows, t1, taps, emb, patch_weight, shared):
    share = shared is not None
    planes = volume_rows.shape[0] + (4 if share else 0)
    whole = lambda shape: pl.BlockSpec(shape, lambda s: (0,) * len(shape))
    weight = patch_weight.reshape(CH, 8, 4, 16, D)
    code, mask = jnp.asarray(second_code()), jnp.asarray(edge_mask(), jnp.bfloat16)
    held = [volume_rows, t1, taps, code, mask, emb]
    in_specs = [whole(array.shape) for array in held]
    in_specs.append(pl.BlockSpec((CH, 1, 4, 16, D), lambda s: (0, jnp.maximum(s - 2, 0), 0, 0, 0)))
    out_specs = [whole((128, D)), whole((128, D))]
    out_shape = [jax.ShapeDtypeStruct((128, D), jnp.bfloat16)] * 2
    scratch = [
        pltpu.VMEM((planes, 144, 128), jnp.float32),
        pltpu.VMEM((3, 512, 640), jnp.bfloat16),
        pltpu.VMEM((128, D), jnp.float32),
        pltpu.VMEM((3, 640, 256), jnp.bfloat16),
    ]
    operands = held + [weight]
    extra = {}
    if share:
        operands += shared
        in_specs += [pl.BlockSpec(memory_space=pl.ANY)] * 2
        out_specs += [pl.BlockSpec(memory_space=pl.ANY)] * 2
        out_shape += [jax.ShapeDtypeStruct((6, D, HD), jnp.bfloat16),
                      jax.ShapeDtypeStruct((8, 256, HD), jnp.bfloat16)]
        scratch += [pltpu.VMEM((2, 2, 64, 128), jnp.bfloat16)]
        scratch += [pltpu.SemaphoreType.DMA((2,))] * 2 + [pltpu.SemaphoreType.DMA((4,))]
        scratch += [pltpu.SemaphoreType.DMA((7, 4))] * 2
        extra = dict(collective_id=1, has_side_effects=True)
    return pl.pallas_call(
        functools.partial(encode_kernel, share),
        grid=(planes - 2,),
        in_specs=in_specs,
        out_specs=out_specs,
        out_shape=out_shape,
        scratch_shapes=scratch,
        compiler_params=pltpu.CompilerParams(vmem_limit_bytes=40 * 2**20, **extra),
        cost_estimate=pl.CostEstimate(flops=8 * 10**9, bytes_accessed=20 * 2**20,
                                      transcendentals=5 * 10**6),
        name="encode",
    )(*operands)


def embed_time(frame_index):
    frequency = jnp.exp(-math.log(1000.0) * jnp.arange(D, dtype=jnp.float32) / D)
    phase_shift = (jnp.arange(D) % 2).astype(jnp.float32) * (math.pi / 2)
    return (jnp.sin(frame_index.astype(jnp.float32)[:, None] * frequency + phase_shift), frequency)


def embed_space(tile_offset, place_x, place_z, place_y, frequency):
    along_x = (tile_offset[0] + EDGE * place_x).astype(jnp.float32)
    along_z = (tile_offset[1] + EDGE * place_z).astype(jnp.float32)
    along_y = (tile_offset[2] + EDGE * place_y).astype(jnp.float32)
    summed = jnp.sin(along_x[:, None, None, None] * frequency) + jnp.sin(
        along_z[None, :, None, None] * frequency + 1.0
    )
    summed = summed + jnp.sin(along_y[None, None, :, None] * frequency + 2.0)
    return summed.reshape(-1, D)


def partners():
    me = lax.axis_index("tm")
    sibling = me + 1 - 2 * (me % 2)
    return me, (sibling, (me + 2) % 4, (sibling + 2) % 4)


def attend_kernel(norm_ref, w_ref, mix_ref, tok_ref, read_ref, out_ref, rows_ref, qkv_ref, att_ref,
                  part_ref, back_ref, send_sem, recv_sem, send_back, recv_back):
    me, others = partners()
    sibling, mirror, diagonal = others
    barrier = pltpu.get_barrier_semaphore()
    for other in others:
        pl.semaphore_signal(barrier, inc=1, device_id={"tm": other},
                            device_id_type=pl.DeviceIdType.MESH)
    pl.semaphore_wait(barrier, 3)

    def rows_copy(src, owner, i, target):
        return pltpu.make_async_remote_copy(
            src_ref=src, dst_ref=rows_ref.at[owner], send_sem=send_sem.at[i],
            recv_sem=recv_sem.at[i], device_id={"tm": target},
            device_id_type=pl.DeviceIdType.MESH)

    to_mirror = rows_copy(norm_ref, me, 1, mirror)
    to_sibling = rows_copy(norm_ref, me, 0, sibling)
    pass_on = rows_copy(rows_ref.at[mirror], mirror, 2, sibling)
    to_mirror.start()
    to_sibling.start()

    def project(block, source):
        rows = source[...]
        for j in range(3):
            pair = jnp.concatenate([w_ref[2 * j], w_ref[2 * j + 1]], axis=1)
            total = jnp.dot(rows, pair, preferred_element_type=jnp.float32)
            qkv_ref[block, :, 256 * j:256 * j + 256] = total.astype(jnp.bfloat16)

    project(me, norm_ref)
    to_sibling.wait_recv()
    project(sibling, rows_ref.at[sibling])
    to_mirror.wait_recv()
    pass_on.start()
    project(mirror, rows_ref.at[mirror])
    pass_on.wait_recv()
    project(diagonal, rows_ref.at[diagonal])

    def back_copy(block, sender, target):
        return pltpu.make_async_remote_copy(
            src_ref=part_ref.at[block], dst_ref=back_ref.at[sender], send_sem=send_back.at[block],
            recv_sem=recv_back.at[sender], device_id={"tm": target},
            device_id_type=pl.DeviceIdType.MESH)

    mixing = jnp.concatenate([mix_ref[i] for i in range(mix_ref.shape[0])], axis=1)
    for block in (3, 0, 2, 1):
        count = 128 * (block + 1)
        for head in range(2):
            lo = head * HD
            query = qkv_ref[block, :, lo:lo + HD]
            keys = qkv_ref[:block + 1, :, 256 + lo:256 + lo + HD].reshape(count, HD)
            values = qkv_ref[:block + 1, :, 512 + lo:512 + lo + HD].reshape(count, HD)
            scores = lax.dot_general(query, keys, (((1,), (1,)), ((), ())),
                                     preferred_element_type=jnp.float32) / math.sqrt(HD)
            row = lax.broadcasted_iota(jnp.int32, (128, count), 0) // 32
            col = lax.broadcasted_iota(jnp.int32, (128, count), 1) // 32
            scores = jnp.where(col <= row + 4 * block, scores, -1e30)
            shifted = jnp.exp(scores - jnp.max(scores, axis=-1, keepdims=True))
            inverse = 1.0 / jnp.sum(shifted, axis=-1, keepdims=True)
            weights = (shifted * inverse).astype(jnp.bfloat16)
            att_ref[block, :, lo:lo + HD] = jnp.dot(
                weights, values, preferred_element_type=jnp.float32).astype(jnp.bfloat16)
        part_ref[block] = jnp.dot(att_ref[block], mixing,
                                  preferred_element_type=jnp.float32).astype(jnp.bfloat16)

        @pl.when(me != block)
        def _():
            back_copy(block, me, block).start()

    residual = tok_ref[...].astype(jnp.float32) + jnp.dot(
        att_ref[me], mixing, preferred_element_type=jnp.float32)
    for other in others:
        back_copy(other, other, other).wait_recv()
        residual += back_ref[other].astype(jnp.float32)
    scale = lax.rsqrt(jnp.mean(residual * residual, axis=-1, keepdims=True) + 1e-05)
    out_ref[...] = jnp.dot((residual * scale).astype(jnp.bfloat16), read_ref[...],
                           preferred_element_type=jnp.float32).astype(jnp.bfloat16)
    for copy in (to_sibling, to_mirror, pass_on):
        copy.wait_send()
    for other in others:
        back_copy(other, me, other).wait_send()


def attend(normed, weights, mixing, token_rows, projector):
    vmem = pl.BlockSpec(memory_space=pltpu.VMEM)
    return pl.pallas_call(
        attend_kernel,
        in_specs=[vmem] * 5,
        out_specs=vmem,
        out_shape=jax.ShapeDtypeStruct((128, projector.shape[1]), jnp.bfloat16),
        scratch_shapes=[
            pltpu.VMEM((4, 128, D), jnp.bfloat16),
            pltpu.VMEM((4, 128, 768), jnp.bfloat16),
            pltpu.VMEM((4, 128, 256), jnp.bfloat16),
            pltpu.VMEM((4, 128, D), jnp.bfloat16),
            pltpu.VMEM((4, 128, D), jnp.bfloat16),
            pltpu.SemaphoreType.DMA((3,)),
            pltpu.SemaphoreType.DMA((3,)),
            pltpu.SemaphoreType.DMA((4,)),
            pltpu.SemaphoreType.DMA((4,)),
        ],
        compiler_params=pltpu.CompilerParams(collective_id=0, has_side_effects=True,
                                             vmem_limit_bytes=32 * 2**20),
        cost_estimate=pl.CostEstimate(flops=10**9, bytes_accessed=4 * 2**20,
                                      transcendentals=4 * 10**5),
        name="attend",
    )(normed, weights, mixing, token_rows, projector)


def head_weights(attend_weight):
    me = lax.axis_index("tm")
    quarter = lax.dynamic_slice_in_dim(attend_weight, me * 256, 256, axis=0)
    quarter = lax.all_gather(quarter, "tile", axis=1, tiled=True)

    def columns(member):
        return jnp.concatenate(
            [lax.dynamic_slice_in_dim(quarter, j * D + member * 256, 256, axis=1) for j in range(3)],
            axis=1)

    me, others = partners()
    weights = jnp.zeros((D, 768), attend_weight.dtype)
    weights = lax.dynamic_update_slice_in_dim(weights, columns(me), me * 256, axis=0)
    for i, other in enumerate(others):
        piece = lax.ppermute(columns(other), "tm", [(m, m ^ (i + 1)) for m in range(4)])
        weights = lax.dynamic_update_slice_in_dim(weights, piece, other * 256, axis=0)
    return weights.reshape(D, 6, HD).transpose(1, 0, 2)


def head_mixing(mixing_weight):
    rows = lax.dynamic_slice_in_dim(mixing_weight, lax.axis_index("tm") * 256, 256, axis=0)
    rows = lax.all_gather(rows, "tile", axis=1, tiled=True)
    return rows.reshape(256, 8, HD).transpose(1, 0, 2)


def local(volume, frame_index, tile_offset, conv_first, conv_second, patch_weight,
          attend_weight, mixing_weight, cube_output_projector):
    frames, width, depth, height = volume.shape
    tile_place = lax.axis_index("tile")
    tiles = lax.axis_size("tile")
    rows = volume.reshape(frames, width, depth // 8, 8, height // 8, 8)
    rows = rows.transpose(1, 3, 5, 0, 2, 4).reshape(width, 64, 128)
    time_emb, frequency = embed_time(frame_index)
    space_emb = embed_space(tile_offset, tile_place + jnp.arange(1), jnp.arange(depth // EDGE),
                            jnp.arange(height // EDGE), frequency)
    emb = (time_emb[:, None, :] + space_emb[None]).reshape(-1, D)
    t1, taps = first_band(conv_first), second_taps(conv_second)
    if tiles == 8 and attend_weight.shape[1] == 3 * HD:
        token_rows, normed, weights, mixing = encode(
            rows, t1, taps, emb, patch_weight, [attend_weight, mixing_weight])
    else:
        from_left = lax.ppermute(rows[-2:], "tile", [(i, i + 1) for i in range(tiles - 1)])
        from_right = lax.ppermute(rows[:2], "tile", [(i + 1, i) for i in range(tiles - 1)])
        rows = jnp.concatenate([from_left, rows, from_right], axis=0)
        token_rows, normed = encode(rows, t1, taps, emb, patch_weight, None)
        weights, mixing = head_weights(attend_weight), head_mixing(mixing_weight)
    prediction = attend(normed, weights, mixing, token_rows, cube_output_projector)
    return prediction.reshape(frames, width // EDGE, depth // EDGE, height // EDGE, -1)


def solution(mesh):
    placed = (P("tm", "tile", None, None), P("tm"), P(), P(), P(), P(), P(None, "tile"),
              P(None, "tile"), P())
    return jax.shard_map(local, mesh=mesh, in_specs=placed,
                         out_specs=P("tm", "tile", None, None, None), check_vma=False)
```

```python
import functools
import math

import jax
import jax.numpy as jnp
import numpy as np
from jax import lax
from jax.experimental import pallas as pl
from jax.experimental.pallas import tpu as pltpu
from jax.sharding import PartitionSpec as P

CH = 16
D = 1024
HEADS = 8
HD = 128
EDGE = 8
TAPS = 3


def window_places():
    zin, yin = [], []
    for pair in range(3):
        zin += [2 * pair] * 8 + [2 * pair + 1] * 8
        yin += list(range(2, 10)) * 2
        zin += [2 * pair + o for o in (0, 0, 1, 1, 1, 1, 0, 0)]
        yin += [10, 11, 0, 1, 10, 11, 0, 1]
    return np.array(zin), np.array(yin)


def map_places():
    zin = [z for z in range(4) for _ in range(8)] + [z for z in range(4) for _ in range(2)]
    yin = [y + 1 for _ in range(4) for y in range(8)] + [0, 9] * 4
    return np.array(zin), np.array(yin)


def banded(row_z, row_y, col_z, col_y, taps):
    dz, dy = row_z - col_z, row_y - col_y
    shared = (dz >= 0) & (dz < TAPS) & (dy >= 0) & (dy < TAPS)
    code = jnp.asarray(np.where(shared, dz * TAPS + dy, -1).astype(np.float32))
    total = 0.0
    for j in range(TAPS):
        for k in range(TAPS):
            total = total + jnp.where(code == float(j * TAPS + k), taps(j, k), 0.0)
    return total


def first_band(conv_first):
    group_z, group_y = map_places()
    row_z, row_y = window_places()
    col_z, col_y = np.repeat(group_z, CH), np.repeat(group_y, CH)
    taps = conv_first.reshape(CH, 27).T.astype(jnp.float32) * 0.5
    spread = jnp.tile(taps, (1, len(group_z))).reshape(3, 3, 3, 1, len(col_z))
    out = banded(row_z[:, None], row_y[:, None], col_z[None], col_y[None],
                 lambda j, k: spread[:, j, k])
    out = out.reshape(3 * len(row_z), -1)
    return jnp.pad(out, ((0, 256 - out.shape[0]), (0, 0))).astype(jnp.bfloat16)


def second_taps(conv_second):
    col = np.arange(256)
    taps = conv_second.transpose(2, 3, 4, 0, 1).reshape(27, CH, CH)
    expand = jnp.asarray((col[None] // 16 == np.arange(CH)[:, None]).astype(np.float32) * 0.5, jnp.bfloat16)
    spread = lax.dot_general(taps, expand, (((1,), (0,)), ((), ())), preferred_element_type=jnp.float32)
    return spread.reshape(27, CH, 256)


def second_code():
    group_z, group_y = map_places()
    col = np.arange(256)
    dz = group_z[:, None] - (col // 8 % 2)[None]
    dy = group_y[:, None] - (col % 8)[None]
    shared = (dz >= 0) & (dz < TAPS) & (dy >= 0) & (dy < TAPS)
    return np.where(shared, dz * TAPS + dy, -1).astype(np.float32).reshape(-1, 1, 256)


def edge_mask():
    p, zc, yc = np.arange(4), np.arange(2), np.arange(16)
    zin, side = np.arange(4), np.arange(2)
    p, _, zc, yc, zin, side, _ = np.meshgrid(
        p, np.arange(4), zc, yc, zin, side, np.arange(CH), indexing="ij")
    bad = (zin == 0) & (p == 0) & (zc == 0)
    bad |= (zin == 3) & (p == 3) & (zc == 1)
    bad |= (side == 0) & (yc == 0)
    bad |= (side == 1) & (yc == 15)
    return np.where(bad, 0.0, 1.0).reshape(512, 128)


def share_steps(step, last, vol_ref, attend_ref, mixing_ref, own_ref, mix_ref, halo_ref, halo_send,
                halo_recv, local_sem, send_sem, recv_sem):
    tile, member = lax.axis_index("tile"), lax.axis_index("tm")
    ends = lax.axis_size("tile") - 1
    row, col = tile // 2, tile % 2
    beside = row * 2 + 1 - col
    column = [((row + d) % 4) * 2 + col for d in (1, 2, 3)]
    far = tile - 1 + 2 * col
    has_far = ((col == 0) & (tile > 0)) | ((col == 1) & (tile < ends))
    mine = pl.ds(pl.multiple_of(member * 256, 256), 256)

    def wanted(owner, j):
        return ((owner * 3 + j) % HEADS) // 2 == member if j < 3 else member >= 0

    def block(owner, j):
        if j == 3:
            return mix_ref.at[owner]
        unit = owner * 3 + j
        return own_ref.at[(unit // HEADS) * 2 + unit % 2]

    def source(j):
        return mixing_ref.at[mine] if j == 3 else attend_ref.at[:, j * HD:(j + 1) * HD]

    def remote(src, owner, kind, j, target):
        return pltpu.make_async_remote_copy(
            src_ref=src, dst_ref=block(owner, j), send_sem=send_sem.at[kind, j],
            recv_sem=recv_sem.at[kind, j], device_id={"tile": target},
            device_id_type=pl.DeviceIdType.MESH)

    def own_copies(j):
        out = [remote(source(j), tile, d, j, column[d - 1]) for d in (1, 2, 3)]
        out.append(remote(source(j), tile, 0, j, beside))
        return out, pltpu.make_async_copy(source(j), block(tile, j), local_sem.at[j])

    def passed_on(d, j):
        owner = ((row - d) % 4) * 2 + col
        return owner, remote(block(owner, j), owner, 3 + d, j, beside)

    def halo(side, target):
        src = vol_ref.at[vol_ref.shape[0] - 2:] if side == 0 else vol_ref.at[:2]
        return pltpu.make_async_remote_copy(
            src_ref=src, dst_ref=halo_ref.at[side], send_sem=halo_send.at[side],
            recv_sem=halo_recv.at[side], device_id={"tile": target},
            device_id_type=pl.DeviceIdType.MESH)

    @pl.when(step == 0)
    def _():
        barrier = pltpu.get_barrier_semaphore()
        for target in [beside] + column:
            pl.semaphore_signal(barrier, inc=1, device_id={"tile": target},
                                device_id_type=pl.DeviceIdType.MESH)

        @pl.when(has_far)
        def _():
            pl.semaphore_signal(barrier, inc=1, device_id={"tile": far},
                                device_id_type=pl.DeviceIdType.MESH)
            pl.semaphore_wait(barrier, 5)

        @pl.when(jnp.logical_not(has_far))
        def _():
            pl.semaphore_wait(barrier, 4)

        @pl.when(tile < ends)
        def _():
            halo(0, tile + 1).start()

        @pl.when(tile > 0)
        def _():
            halo(1, tile - 1).start()

        for way, fits in ((3, row >= 0), (0, row < 3), (2, row > 0), (1, row >= 0),
                          (0, row == 3), (2, row == 0)):
            for j in range(4):
                @pl.when(wanted(tile, j) & fits)
                def _():
                    own_copies(j)[0][way].start()

        for j in range(4):
            @pl.when(wanted(tile, j))
            def _():
                own_copies(j)[1].start()

        @pl.when(tile > 0)
        def _():
            halo(0, tile - 1).wait_recv()

        @pl.when(tile == 0)
        def _():
            halo_ref[0] = jnp.zeros(halo_ref.shape[1:], halo_ref.dtype)

        @pl.when(tile < ends)
        def _():
            halo(1, tile + 1).wait_recv()

        @pl.when(tile == ends)
        def _():
            halo_ref[1] = jnp.zeros(halo_ref.shape[1:], halo_ref.dtype)

    for d, when, fits in ((1, 3, row > 0), (3, 4, row < 3), (2, 6, row >= 0), (1, 8, row == 0),
                          (3, 8, row == 3)):
        @pl.when(step == when)
        def _():
            for j in range(4):
                owner, onward = passed_on(d, j)

                @pl.when(wanted(owner, j) & fits)
                def _():
                    remote(source(j), owner, d, j, beside).wait_recv()
                    onward.start()

    @pl.when(step == last)
    def _():
        @pl.when(tile < ends)
        def _():
            halo(0, tile + 1).wait_send()

        @pl.when(tile > 0)
        def _():
            halo(1, tile - 1).wait_send()

        for j in range(4):
            @pl.when(wanted(tile, j))
            def _():
                copies, here = own_copies(j)
                for copy in copies:
                    copy.wait_send()
                here.wait()

            for d in (1, 2, 3):
                owner, onward = passed_on(d, j)

                @pl.when(wanted(owner, j))
                def _():
                    onward.wait_send()

            for kind, back in ((0, 0), (4, 1), (5, 2), (6, 3)):
                owner = ((row - back) % 4) * 2 + 1 - col

                @pl.when(wanted(owner, j))
                def _():
                    remote(source(j), owner, kind, j, beside).wait_recv()


def encode_kernel(share, *refs):
    vol_ref, t1_ref, taps_ref, code_ref, mask_ref, emb_ref, w_ref = refs[:7]
    if share:
        attend_ref, mixing_ref, tok_ref, norm_ref, own_ref, mix_ref = refs[7:13]
        win_ref, maps_ref, acc_ref, t2_ref, halo_ref = refs[13:18]
    else:
        tok_ref, norm_ref, win_ref, maps_ref, acc_ref, t2_ref = refs[7:]
    step = pl.program_id(0)
    last = pl.num_programs(0) - 1
    if share:
        share_steps(step, last, vol_ref, attend_ref, mixing_ref, own_ref, mix_ref, halo_ref, *refs[18:])

    @pl.when(step == 0)
    def _():
        acc_ref[...] = jnp.zeros_like(acc_ref)

        @pl.loop(0, code_ref.shape[0])
        def _(group):
            code = code_ref[group]
            for dx in range(3):
                total = jnp.zeros((CH, 256), jnp.float32)
                for tap in range(9):
                    total += jnp.where(code == float(tap), taps_ref[9 * dx + tap], 0.0)
                t2_ref[dx, pl.ds(pl.multiple_of(group * CH, CH), CH)] = total.astype(jnp.bfloat16)

        row = lax.broadcasted_iota(jnp.int32, (96, 128), 0) % 8
        lane = lax.broadcasted_iota(jnp.int32, (96, 128), 1)
        up_ok = (row >= 6) & (lane % 16 >= 1)
        down_ok = (row < 2) & (lane % 16 <= 14)
        zc = lax.broadcasted_iota(jnp.int32, (16, 128), 1) // 16 % 2

        def window_plane(x, plane):
            here = plane.astype(jnp.float32)
            below = jnp.where(zc == 1, pltpu.roll(here[48:], 16, 1), 0.0)
            above = jnp.where(zc == 0, pltpu.roll(here[:16], 112, 1), 0.0)
            planes = jnp.concatenate([below, here, above], axis=0)
            halo = jnp.where(up_ok, pltpu.roll(planes, 1, 1), 0.0)
            halo = halo + jnp.where(down_ok, pltpu.roll(planes, 127, 1), 0.0)
            for q in range(6):
                win_ref[x, 24 * q:24 * q + 16] = planes[16 * q:16 * q + 16]
                win_ref[x, 24 * q + 16:24 * q + 24] = halo[16 * q:16 * q + 8] + pltpu.roll(
                    halo[16 * q + 8:16 * q + 16], 4, 0)

        @pl.loop(0, vol_ref.shape[0])
        def _(x):
            window_plane(x + (2 if share else 0), vol_ref[x])

        if share:
            @pl.loop(0, 2)
            def _(x):
                window_plane(x, halo_ref[0, x])
                window_plane(vol_ref.shape[0] + 2 + x, halo_ref[1, x])

    slot = step % 3
    parts = []
    for p in range(4):
        rows = [win_ref[step + d, 24 * p:24 * p + 72] for d in range(3)]
        window = jnp.concatenate(rows + [jnp.zeros((40, 128), jnp.float32)], axis=0)
        parts.append(window.T.astype(jnp.bfloat16))
    window = jnp.concatenate(parts, axis=0)
    for lo, hi in ((0, 256), (256, 512), (512, 640)):
        half = jnp.dot(window, t1_ref[:, lo:hi], preferred_element_type=jnp.float32)
        maps = (half + half * jnp.tanh(half)).astype(jnp.bfloat16)
        if lo == 512:
            maps = maps * mask_ref[...]
        maps_ref[slot, :, lo:hi] = maps
    none = jnp.zeros((16, 128), jnp.bfloat16)
    for t in range(4):
        maps_ref[slot, 32 * t:32 * t + 16, 0:128] = none
        maps_ref[slot, 400 + 32 * t:416 + 32 * t, 384:512] = none

    tile = lax.axis_index("tile")
    outside = ((step == 0) & (tile == 0)) | ((step == last) & (tile == lax.axis_size("tile") - 1))

    @pl.when(outside)
    def _():
        maps_ref[slot] = jnp.zeros(maps_ref.shape[1:], jnp.bfloat16)

    @pl.when(step >= 2)
    def _():
        half = jnp.dot(maps_ref[(step + 1) % 3], t2_ref[0], preferred_element_type=jnp.float32)
        half += jnp.dot(maps_ref[(step + 2) % 3], t2_ref[1], preferred_element_type=jnp.float32)
        half += jnp.dot(maps_ref[slot], t2_ref[2], preferred_element_type=jnp.float32)
        second = (half + half * jnp.tanh(half)).astype(jnp.bfloat16)
        total = acc_ref[...]
        for p in range(4):
            weight = w_ref[:, 0, p].reshape(256, D)
            total += jnp.dot(second[128 * p:128 * p + 128], weight, preferred_element_type=jnp.float32)
        acc_ref[...] = total

    @pl.when(step == last)
    def _():
        tokens = (acc_ref[...] + emb_ref[...]).astype(jnp.bfloat16)
        tok_ref[...] = tokens
        wide = tokens.astype(jnp.float32)
        scale = lax.rsqrt(jnp.mean(wide * wide, axis=-1, keepdims=True) + 1e-05)
        norm_ref[...] = (wide * scale).astype(jnp.bfloat16)


def encode(volume_rows, t1, taps, emb, patch_weight, shared):
    share = shared is not None
    planes = volume_rows.shape[0] + (4 if share else 0)
    whole = lambda shape: pl.BlockSpec(shape, lambda s: (0,) * len(shape))
    weight = patch_weight.reshape(CH, 8, 4, 16, D)
    code, mask = jnp.asarray(second_code()), jnp.asarray(edge_mask(), jnp.bfloat16)
    held = [volume_rows, t1, taps, code, mask, emb]
    in_specs = [whole(array.shape) for array in held]
    in_specs.append(pl.BlockSpec((CH, 1, 4, 16, D), lambda s: (0, jnp.maximum(s - 2, 0), 0, 0, 0)))
    out_specs = [whole((128, D)), whole((128, D))]
    out_shape = [jax.ShapeDtypeStruct((128, D), jnp.bfloat16)] * 2
    scratch = [
        pltpu.VMEM((planes, 144, 128), jnp.float32),
        pltpu.VMEM((3, 512, 640), jnp.bfloat16),
        pltpu.VMEM((128, D), jnp.float32),
        pltpu.VMEM((3, 640, 256), jnp.bfloat16),
    ]
    operands = held + [weight]
    extra = {}
    if share:
        operands += shared
        in_specs += [pl.BlockSpec(memory_space=pl.ANY)] * 2
        out_specs += [pl.BlockSpec(memory_space=pl.ANY)] * 2
        out_shape += [jax.ShapeDtypeStruct((6, D, HD), jnp.bfloat16),
                      jax.ShapeDtypeStruct((8, 256, HD), jnp.bfloat16)]
        scratch += [pltpu.VMEM((2, 2, 64, 128), jnp.bfloat16)]
        scratch += [pltpu.SemaphoreType.DMA((2,))] * 2 + [pltpu.SemaphoreType.DMA((4,))]
        scratch += [pltpu.SemaphoreType.DMA((7, 4))] * 2
        extra = dict(collective_id=1, has_side_effects=True)
    return pl.pallas_call(
        functools.partial(encode_kernel, share),
        grid=(planes - 2,),
        in_specs=in_specs,
        out_specs=out_specs,
        out_shape=out_shape,
        scratch_shapes=scratch,
        compiler_params=pltpu.CompilerParams(vmem_limit_bytes=40 * 2**20, **extra),
        cost_estimate=pl.CostEstimate(flops=8 * 10**9, bytes_accessed=20 * 2**20,
                                      transcendentals=5 * 10**6),
        name="encode",
    )(*operands)


def embed_time(frame_index):
    frequency = jnp.exp(-math.log(1000.0) * jnp.arange(D, dtype=jnp.float32) / D)
    phase_shift = (jnp.arange(D) % 2).astype(jnp.float32) * (math.pi / 2)
    return (jnp.sin(frame_index.astype(jnp.float32)[:, None] * frequency + phase_shift), frequency)


def embed_space(tile_offset, place_x, place_z, place_y, frequency):
    along_x = (tile_offset[0] + EDGE * place_x).astype(jnp.float32)
    along_z = (tile_offset[1] + EDGE * place_z).astype(jnp.float32)
    along_y = (tile_offset[2] + EDGE * place_y).astype(jnp.float32)
    summed = jnp.sin(along_x[:, None, None, None] * frequency) + jnp.sin(
        along_z[None, :, None, None] * frequency + 1.0
    )
    summed = summed + jnp.sin(along_y[None, None, :, None] * frequency + 2.0)
    return summed.reshape(-1, D)


def partners():
    me = lax.axis_index("tm")
    sibling = me + 1 - 2 * (me % 2)
    return me, (sibling, (me + 2) % 4, (sibling + 2) % 4)


def attend_kernel(norm_ref, w_ref, mix_ref, tok_ref, read_ref, out_ref, rows_ref, qkv_ref, att_ref,
                  part_ref, back_ref, send_sem, recv_sem, send_back, recv_back):
    me, others = partners()
    sibling, mirror, diagonal = others
    barrier = pltpu.get_barrier_semaphore()
    for other in others:
        pl.semaphore_signal(barrier, inc=1, device_id={"tm": other},
                            device_id_type=pl.DeviceIdType.MESH)
    pl.semaphore_wait(barrier, 3)

    def rows_copy(src, owner, i, target):
        return pltpu.make_async_remote_copy(
            src_ref=src, dst_ref=rows_ref.at[owner], send_sem=send_sem.at[i],
            recv_sem=recv_sem.at[i], device_id={"tm": target},
            device_id_type=pl.DeviceIdType.MESH)

    to_mirror = rows_copy(norm_ref, me, 1, mirror)
    to_sibling = rows_copy(norm_ref, me, 0, sibling)
    pass_on = rows_copy(rows_ref.at[mirror], mirror, 2, sibling)
    to_mirror.start()
    to_sibling.start()

    def project(block, source):
        rows = source[...]
        for j in range(3):
            pair = jnp.concatenate([w_ref[2 * j], w_ref[2 * j + 1]], axis=1)
            total = jnp.dot(rows, pair, preferred_element_type=jnp.float32)
            qkv_ref[block, :, 256 * j:256 * j + 256] = total.astype(jnp.bfloat16)

    project(me, norm_ref)
    to_sibling.wait_recv()
    project(sibling, rows_ref.at[sibling])
    to_mirror.wait_recv()
    pass_on.start()
    project(mirror, rows_ref.at[mirror])
    pass_on.wait_recv()
    project(diagonal, rows_ref.at[diagonal])

    def back_copy(block, sender, target):
        return pltpu.make_async_remote_copy(
            src_ref=part_ref.at[block], dst_ref=back_ref.at[sender], send_sem=send_back.at[block],
            recv_sem=recv_back.at[sender], device_id={"tm": target},
            device_id_type=pl.DeviceIdType.MESH)

    mixing = jnp.concatenate([mix_ref[i] for i in range(mix_ref.shape[0])], axis=1)
    for block in (3, 0, 2, 1):
        count = 128 * (block + 1)
        for head in range(2):
            lo = head * HD
            query = qkv_ref[block, :, lo:lo + HD]
            keys = qkv_ref[:block + 1, :, 256 + lo:256 + lo + HD].reshape(count, HD)
            values = qkv_ref[:block + 1, :, 512 + lo:512 + lo + HD].reshape(count, HD)
            scores = lax.dot_general(query, keys, (((1,), (1,)), ((), ())),
                                     preferred_element_type=jnp.float32) / math.sqrt(HD)
            row = lax.broadcasted_iota(jnp.int32, (128, count), 0) // 32
            col = lax.broadcasted_iota(jnp.int32, (128, count), 1) // 32
            scores = jnp.where(col <= row + 4 * block, scores, -1e30)
            shifted = jnp.exp(scores - jnp.max(scores, axis=-1, keepdims=True))
            inverse = 1.0 / jnp.sum(shifted, axis=-1, keepdims=True)
            weights = (shifted * inverse).astype(jnp.bfloat16)
            att_ref[block, :, lo:lo + HD] = jnp.dot(
                weights, values, preferred_element_type=jnp.float32).astype(jnp.bfloat16)
        part_ref[block] = jnp.dot(att_ref[block], mixing,
                                  preferred_element_type=jnp.float32).astype(jnp.bfloat16)

        @pl.when(me != block)
        def _():
            back_copy(block, me, block).start()

    residual = tok_ref[...].astype(jnp.float32) + jnp.dot(
        att_ref[me], mixing, preferred_element_type=jnp.float32)
    for other in others:
        back_copy(other, other, other).wait_recv()
        residual += back_ref[other].astype(jnp.float32)
    scale = lax.rsqrt(jnp.mean(residual * residual, axis=-1, keepdims=True) + 1e-05)
    out_ref[...] = jnp.dot((residual * scale).astype(jnp.bfloat16), read_ref[...],
                           preferred_element_type=jnp.float32).astype(jnp.bfloat16)
    for copy in (to_sibling, to_mirror, pass_on):
        copy.wait_send()
    for other in others:
        back_copy(other, me, other).wait_send()


def attend(normed, weights, mixing, token_rows, projector):
    vmem = pl.BlockSpec(memory_space=pltpu.VMEM)
    return pl.pallas_call(
        attend_kernel,
        in_specs=[vmem] * 5,
        out_specs=vmem,
        out_shape=jax.ShapeDtypeStruct((128, projector.shape[1]), jnp.bfloat16),
        scratch_shapes=[
            pltpu.VMEM((4, 128, D), jnp.bfloat16),
            pltpu.VMEM((4, 128, 768), jnp.bfloat16),
            pltpu.VMEM((4, 128, 256), jnp.bfloat16),
            pltpu.VMEM((4, 128, D), jnp.bfloat16),
            pltpu.VMEM((4, 128, D), jnp.bfloat16),
            pltpu.SemaphoreType.DMA((3,)),
            pltpu.SemaphoreType.DMA((3,)),
            pltpu.SemaphoreType.DMA((4,)),
            pltpu.SemaphoreType.DMA((4,)),
        ],
        compiler_params=pltpu.CompilerParams(collective_id=0, has_side_effects=True,
                                             vmem_limit_bytes=32 * 2**20),
        cost_estimate=pl.CostEstimate(flops=10**9, bytes_accessed=4 * 2**20,
                                      transcendentals=4 * 10**5),
        name="attend",
    )(normed, weights, mixing, token_rows, projector)


def head_weights(attend_weight):
    me = lax.axis_index("tm")
    quarter = lax.dynamic_slice_in_dim(attend_weight, me * 256, 256, axis=0)
    quarter = lax.all_gather(quarter, "tile", axis=1, tiled=True)

    def columns(member):
        return jnp.concatenate(
            [lax.dynamic_slice_in_dim(quarter, j * D + member * 256, 256, axis=1) for j in range(3)],
            axis=1)

    me, others = partners()
    weights = jnp.zeros((D, 768), attend_weight.dtype)
    weights = lax.dynamic_update_slice_in_dim(weights, columns(me), me * 256, axis=0)
    for i, other in enumerate(others):
        piece = lax.ppermute(columns(other), "tm", [(m, m ^ (i + 1)) for m in range(4)])
        weights = lax.dynamic_update_slice_in_dim(weights, piece, other * 256, axis=0)
    return weights.reshape(D, 6, HD).transpose(1, 0, 2)


def head_mixing(mixing_weight):
    rows = lax.dynamic_slice_in_dim(mixing_weight, lax.axis_index("tm") * 256, 256, axis=0)
    rows = lax.all_gather(rows, "tile", axis=1, tiled=True)
    return rows.reshape(256, 8, HD).transpose(1, 0, 2)


def local(volume, frame_index, tile_offset, conv_first, conv_second, patch_weight,
          attend_weight, mixing_weight, cube_output_projector):
    frames, width, depth, height = volume.shape
    tile_place = lax.axis_index("tile")
    tiles = lax.axis_size("tile")
    rows = volume.reshape(frames, width, depth // 8, 8, height // 8, 8)
    rows = rows.transpose(1, 3, 5, 0, 2, 4).reshape(width, 64, 128)
    time_emb, frequency = embed_time(frame_index)
    space_emb = embed_space(tile_offset, tile_place + jnp.arange(1), jnp.arange(depth // EDGE),
                            jnp.arange(height // EDGE), frequency)
    emb = (time_emb[:, None, :] + space_emb[None]).reshape(-1, D)
    t1, taps = first_band(conv_first), second_taps(conv_second)
    if tiles == 8 and attend_weight.shape[1] == 3 * HD:
        token_rows, normed, weights, mixing = encode(
            rows, t1, taps, emb, patch_weight, [attend_weight, mixing_weight])
    else:
        from_left = lax.ppermute(rows[-2:], "tile", [(i, i + 1) for i in range(tiles - 1)])
        from_right = lax.ppermute(rows[:2], "tile", [(i + 1, i) for i in range(tiles - 1)])
        rows = jnp.concatenate([from_left, rows, from_right], axis=0)
        token_rows, normed = encode(rows, t1, taps, emb, patch_weight, None)
        weights, mixing = head_weights(attend_weight), head_mixing(mixing_weight)
    prediction = attend(normed, weights, mixing, token_rows, cube_output_projector)
    return prediction.reshape(frames, width // EDGE, depth // EDGE, height // EDGE, -1)


def solution(mesh):
    placed = (P("tm", "tile", None, None), P("tm"), P(), P(), P(), P(), P(None, "tile"),
              P(None, "tile"), P())
    return jax.shard_map(local, mesh=mesh, in_specs=placed,
                         out_specs=P("tm", "tile", None, None, None), check_vma=False)
```
